32 devices in a mesh: groups: 2 (over x), hid: 16 (over z, y, core).
Axes of the slice: x: 2, y: 2, z: 4, core: 2. Of those that a mesh axis runs over, the one named last changes fastest.
Arguments:
- queries: bfloat16 [128, 64, 128], P(('groups', 'hid')), parts along dimension 0, may hold values from -12 to 12
- k_cache: bfloat16 [128, 192, 1024], P(('groups', 'hid')), parts along dimension 0, may hold values from -450 to 450
- v_cache: bfloat16 [128, 192, 1024], P(('groups', 'hid')), parts along dimension 0, may hold values from -6 to 6
- lengths: int32 [128], P(('groups', 'hid')), parts along dimension 0, may hold values from 24 to 192, as said below
- residual_in: bfloat16 [128, 8192], P(('groups', 'hid')), parts along dimension 0, may hold values from -6 to 6
- norm_gain: float32 [8192], replicated, may hold values from 0.25 to 1.75
- gate_w: bfloat16 [16, 56, 1024, 128], P('hid'), may hold values from -0.0625 to 0.0625
- up_w: bfloat16 [16, 56, 1024, 128], P('hid'), may hold values from -0.0625 to 0.0625
- down_w: bfloat16 [16, 56, 128, 1024], P('hid'), may hold values from -0.09375 to 0.09375
- block_list: int32 [4, 28], P('groups'), parts along dimension 0, may hold values from 0 to 55, as said below
- block_count: int32 [4], P('groups'), parts along dimension 0, may hold values from 1 to 28, as said below
Outputs:
- layer_out: bfloat16 [128, 8192], P(('groups', 'hid')), parts along dimension 0
The draws below stay inside these ranges and needn't reach their ends.
There are 2 independent parts, one for each index of `groups`. The reference program is written for one: setup_inputs(seed, part) draws one part's arguments, and reference() takes and returns one part's arrays. A program takes and returns all parts, laid end to end along the dimension named above; an argument that names none is the same for every part. Nothing has to cross between parts.
Inputs may be any that keep to these rules, and one draw needn't show every extreme that they name: `lengths`: some request's length is 192. `block_list`: each row holds 28 distinct block indices of its group. `block_count`: exactly one group has all 28 listed blocks active.
All inputs are finite; a program needn't handle non-finite values.
Results may differ from the reference program's by a relative error of at most 0.006.
Values may be sent and summed in bfloat16 or wider, within the bound.
No kernel may reach another device: no remote copies, remote signals or barrier semaphores. Data moves between devices by JAX's collectives and lax.ppermute only.
A program may use at most 128 MiB of HBM per device.

```python
import math
import jax
import jax.numpy as jnp
from jax import lax

D = 8192
H = 64
KV = 8
HD = 128
BW = 128
MDL = 8
REQ_DEV = 4
CACHE = 192
HG = 2
DS = 1024
BLK_G = 56
CAP = 28
BATCH = 64
N_HID = 16


def query_key_pair(key):
    query_stream = jax.random.fold_in(key, 11)
    cache_stream = jax.random.fold_in(key, 12)
    query_vals = jnp.clip(jax.random.normal(query_stream, (BATCH, H, HD), jnp.float32), -6.0, 6.0)
    key_vals = jnp.clip(jax.random.normal(cache_stream, (BATCH, CACHE, KV, HD), jnp.float32), -6.0, 6.0)
    return (query_vals, key_vals.reshape(BATCH, CACHE, KV * HD))


def draw_queries(key, part):
    return query_key_pair(key)[0].astype(jnp.bfloat16)


def draw_k_cache(key, part):
    return query_key_pair(key)[1].astype(jnp.bfloat16)


def draw_lengths(key, part):
    length_stream = jax.random.fold_in(key, 21)
    drawn = jax.random.randint(length_stream, (BATCH,), max(2, CACHE // 8), CACHE + 1, jnp.int32)
    full_row = jax.random.randint(jax.random.fold_in(length_stream, 1), (), 0, BATCH, jnp.int32)
    return jnp.where(jnp.arange(BATCH, dtype=jnp.int32) == full_row, CACHE, drawn).astype(jnp.int32)


def draw_block_list(key, part):
    table_stream = jax.random.fold_in(key, 31)
    row_streams = jax.random.split(table_stream, HG)
    rows_all = jax.vmap(lambda stream: jax.random.permutation(stream, BLK_G)[:CAP])(row_streams).astype(jnp.int32)
    first_row = rows_all[0]
    held = first_row[0]
    first_row = jnp.where(first_row == BLK_G - 1, held, first_row)
    first_row = first_row.at[0].set(BLK_G - 1)
    second = first_row[1]
    first_row = jnp.where(first_row == 0, second, first_row)
    first_row = first_row.at[1].set(0)
    return rows_all.at[0].set(first_row)


def draw_block_count(key, part):
    count_stream = jax.random.fold_in(key, 47)
    counts = jax.random.randint(jax.random.fold_in(count_stream, 3), (HG,), 1, CAP, jnp.int32)
    full_group = jax.random.randint(jax.random.fold_in(count_stream, 5), (), 0, HG, jnp.int32)
    return jnp.where(jnp.arange(HG, dtype=jnp.int32) == full_group, CAP, counts).astype(jnp.int32)


def levels(own_key, extent, pieces, low, high):
    loudness = 1.0
    for axis_at, blocks in pieces:
        draws = jax.random.uniform(jax.random.fold_in(jax.random.fold_in(own_key, 6), axis_at), (blocks,), jnp.float32, low / len(pieces), high / len(pieces))
        loudness = loudness * jnp.repeat(jnp.exp(draws), extent[axis_at] // blocks).reshape((-1,) + (1,) * (len(extent) - 1 - axis_at))
    return loudness


def gaussian(own_key, extent, deviation, most, cuts=(), kind=jnp.bfloat16):
    loudness = levels(own_key, extent, cuts, -0.22, 0.18) if cuts else 1.0
    array = jax.random.normal(own_key, extent, jnp.float32) * deviation * loudness
    return jnp.minimum(jnp.maximum(array, -most), most).astype(kind)


def setup_inputs(seed: int = 0, part: int = 0) -> dict:
    streams_of = jax.random.split(jax.random.key(seed), 12)
    part_splits = jax.random.split(jax.random.fold_in(streams_of[11], part), 12)
    queries = draw_queries(jax.random.fold_in(jax.random.fold_in(streams_of[11], part), 71), part)
    k_cache = draw_k_cache(jax.random.fold_in(jax.random.fold_in(streams_of[11], part), 71), part)
    v_cache = gaussian(part_splits[2], (BATCH, CACHE, KV * HD), 1.0, 6.0, ((0, 16),))
    lengths = draw_lengths(jax.random.fold_in(jax.random.fold_in(streams_of[11], part), 71), part)
    residual_in = gaussian(part_splits[4], (BATCH, D), 1.0, 6.0, ((0, 16),))
    norm_gain = jnp.clip(1.0 + 0.15 * jax.random.normal(streams_of[5], (D,), jnp.float32), 0.25, 1.75)
    gate_w = gaussian(streams_of[6], (N_HID, BLK_G, DS, BW), D ** -0.5, 0.0625, ((0, 16),))
    up_w = gaussian(streams_of[7], (N_HID, BLK_G, DS, BW), D ** -0.5, 0.0625, ((0, 16),))
    down_w = gaussian(streams_of[8], (N_HID, BLK_G, BW, DS), (CAP * BW * HG // 2) ** -0.5, 0.09375, ((0, 16),))
    block_list = draw_block_list(jax.random.fold_in(jax.random.fold_in(streams_of[11], part), 71), part)
    block_count = draw_block_count(jax.random.fold_in(jax.random.fold_in(streams_of[11], part), 71), part)
    return dict(queries=queries, k_cache=k_cache, v_cache=v_cache, lengths=lengths, residual_in=residual_in, norm_gain=norm_gain, gate_w=gate_w, up_w=up_w, down_w=down_w, block_list=block_list, block_count=block_count)


def attend_block(parts):
    query_part, key_part, value_part, length_part = parts
    rows_here = query_part.shape[0]
    query_f = query_part.astype(jnp.float32).reshape(rows_here, KV, H // KV, HD)
    key_f = key_part.astype(jnp.float32).reshape(rows_here, CACHE, KV, HD)
    value_f = value_part.astype(jnp.float32).reshape(rows_here, CACHE, KV, HD)
    scores = jnp.einsum('rkgd,rtkd->rkgt', query_f, key_f) / math.sqrt(HD)
    valid = jnp.arange(CACHE)[None, None, None, :] < length_part[:, None, None, None]
    scores = jnp.where(valid, scores, -1e+30)
    row_top = lax.optimization_barrier(jnp.max(scores, axis=-1, keepdims=True))
    exp_terms = jnp.where(valid, jnp.exp(scores - row_top), 0.0)
    attn_probs = (exp_terms / lax.optimization_barrier(jnp.sum(exp_terms, axis=-1, keepdims=True))).astype(jnp.bfloat16)
    attended = jnp.einsum('rkgt,rtkd->rkgd', attn_probs.astype(jnp.float32), value_f)
    return attended.reshape(rows_here, D)

def select_blocks(tiles, block_list):
    return jax.vmap(lambda tile_set, chosen: jnp.take(tile_set, chosen, axis=1))(tiles, block_list)

def reference(queries, k_cache, v_cache, lengths, residual_in, norm_gain, gate_w, up_w, down_w, block_list, block_count):
    attended = lax.map(attend_block, (queries.reshape(N_HID, REQ_DEV, H, HD), k_cache.reshape(N_HID, REQ_DEV, CACHE, KV * HD), v_cache.reshape(N_HID, REQ_DEV, CACHE, KV * HD), lengths.reshape(N_HID, REQ_DEV))).reshape(BATCH, D)
    mixed_rows = residual_in.astype(jnp.float32) + attended
    mean_sq = lax.optimization_barrier(jnp.mean(mixed_rows * mixed_rows, axis=1, keepdims=True))
    normed = (mixed_rows * lax.rsqrt(mean_sq + 1e-05) * norm_gain).astype(jnp.bfloat16)
    normed_f = normed.astype(jnp.float32).reshape(BATCH, MDL, DS)
    gate_sel = select_blocks(gate_w.reshape(HG, MDL, BLK_G, DS, BW), block_list).astype(jnp.float32)
    up_sel = select_blocks(up_w.reshape(HG, MDL, BLK_G, DS, BW), block_list).astype(jnp.float32)
    down_sel = select_blocks(down_w.reshape(HG, MDL, BLK_G, BW, DS), block_list).astype(jnp.float32)
    gate_pre = jnp.einsum('bms,gmcsu->bgcu', normed_f, gate_sel)
    up_pre = jnp.einsum('bms,gmcsu->bgcu', normed_f, up_sel)
    active = jnp.arange(CAP)[None, :] < block_count[:, None]
    hidden = jnp.where(active[None, :, :, None], jnp.maximum(gate_pre, 0.0) * up_pre, 0.0).astype(jnp.bfloat16)
    ffn_out = jnp.einsum('bgcu,gmcus->bms', hidden.astype(jnp.float32), down_sel).reshape(BATCH, D)
    return (mixed_rows + ffn_out).astype(jnp.bfloat16)
```

```python
import functools
import math

import jax
import jax.numpy as jnp
from jax import lax
from jax.experimental import pallas as pl
from jax.experimental.pallas import tpu as pltpu
from jax.sharding import PartitionSpec as P

MDL = 8
VMEM = pl.BlockSpec(memory_space=pltpu.VMEM)
SMEM = pl.BlockSpec(memory_space=pltpu.SMEM)
ANY = pl.BlockSpec(memory_space=pl.ANY)


def from_partner(value, apart):
    mask = 2**apart
    pairs = [(source, source ^ mask) for source in range(lax.axis_size("hid"))]
    return lax.ppermute(value, "hid", pairs)


def attend_kernel(
    kv_count, len_ref, q_ref, k_hbm, v_hbm, res_ref, gain_ref, mixed_ref, send_ref, k_buf, v_buf, sems
):
    rows, heads, size = q_ref.shape
    slots = k_buf.shape[1]
    width = kv_count * size
    per_kv = heads // kv_count
    k_copies = [pltpu.make_async_copy(k_hbm.at[r], k_buf.at[r], sems.at[0, r]) for r in range(rows)]
    v_copies = [pltpu.make_async_copy(v_hbm.at[r], v_buf.at[r], sems.at[1, r]) for r in range(rows)]
    for r in range(rows):
        k_copies[r].start()
        v_copies[r].start()
    own = (
        lax.broadcasted_iota(jnp.int32, (heads, width), 0) // per_kv
        == lax.broadcasted_iota(jnp.int32, (heads, width), 1) // size
    )
    slot_at = lax.broadcasted_iota(jnp.int32, (heads, slots), 1)
    for r in range(rows):
        wide = jnp.concatenate([q_ref[r]] * kv_count, axis=1)
        wide = jnp.where(own, wide, jnp.zeros_like(wide))
        k_copies[r].wait()
        scores = lax.dot_general(
            wide, k_buf[r], (((1,), (1,)), ((), ())), preferred_element_type=jnp.float32
        ) * (1.0 / math.sqrt(size))
        valid = slot_at < len_ref[r]
        scores = jnp.where(valid, scores, -1e30)
        top = jnp.max(scores, axis=1, keepdims=True)
        terms = jnp.where(valid, jnp.exp(scores - top), 0.0)
        probs = (terms / jnp.sum(terms, axis=1, keepdims=True)).astype(jnp.bfloat16)
        v_copies[r].wait()
        out = jnp.dot(probs, v_buf[r], preferred_element_type=jnp.float32)
        for h in range(heads):
            at = h // per_kv * size
            mixed_ref[r : r + 1, h * size : (h + 1) * size] = out[h : h + 1, at : at + size]
    mixed = mixed_ref[...] + res_ref[...].astype(jnp.float32)
    mixed_ref[...] = mixed
    mean_sq = jnp.mean(mixed * mixed, axis=1, keepdims=True)
    normed = (mixed * lax.rsqrt(mean_sq + 1e-05) * gain_ref[...]).astype(jnp.bfloat16)
    step = send_ref.shape[2]
    for m in range(MDL):
        part = normed[:, m * step : (m + 1) * step]
        for g in range(send_ref.shape[0] // MDL):
            send_ref[g * MDL + m] = part


def attend(queries, k_cache, v_cache, lengths, residual_in, norm_gain, dev_count):
    rows, heads, size = queries.shape
    slots, width = k_cache.shape[1:]
    model = residual_in.shape[1]
    return pl.pallas_call(
        functools.partial(attend_kernel, width // size),
        out_shape=(
            jax.ShapeDtypeStruct((rows, model), jnp.float32),
            jax.ShapeDtypeStruct((dev_count, rows, model // MDL), jnp.bfloat16),
        ),
        in_specs=[SMEM, VMEM, ANY, ANY, VMEM, VMEM],
        out_specs=(VMEM, VMEM),
        scratch_shapes=[
            pltpu.VMEM((rows, slots, width), jnp.bfloat16),
            pltpu.VMEM((rows, slots, width), jnp.bfloat16),
            pltpu.SemaphoreType.DMA((2, rows)),
        ],
        compiler_params=pltpu.CompilerParams(vmem_limit_bytes=16 * 2**20),
        name="attend",
    )(lengths, queries, k_cache, v_cache, residual_in, norm_gain.reshape(1, model))


def fetch_in_kernel(list_ref, gate_hbm, up_hbm, both_ref, sems):
    group = lax.axis_index("hid") // MDL
    count, _, twice = both_ref.shape
    unit = twice // 2

    def copies(c):
        block = list_ref[group, c]
        return (
            pltpu.make_async_copy(gate_hbm.at[0, block], both_ref.at[c, :, pl.ds(0, unit)], sems.at[0, c]),
            pltpu.make_async_copy(up_hbm.at[0, block], both_ref.at[c, :, pl.ds(unit, unit)], sems.at[1, c]),
        )

    @pl.loop(0, count)
    def _(c):
        for copy in copies(c):
            copy.start()

    @pl.loop(0, count)
    def _(c):
        for copy in copies(c):
            copy.wait()


def fetch_in(block_list, gate_w, up_w):
    count = block_list.shape[1]
    depth, unit = gate_w.shape[2:]
    return pl.pallas_call(
        fetch_in_kernel,
        out_shape=jax.ShapeDtypeStruct((count, depth, 2 * unit), jnp.bfloat16),
        in_specs=[SMEM, ANY, ANY],
        out_specs=VMEM,
        scratch_shapes=[pltpu.SemaphoreType.DMA((2, count))],
        compiler_params=pltpu.CompilerParams(vmem_limit_bytes=20 * 2**20),
        cost_estimate=pl.CostEstimate(flops=0, bytes_accessed=4 * count * depth * unit * 2, transcendentals=0),
        name="fetch_in",
    )(block_list, gate_w, up_w)


def fetch_down_kernel(list_ref, down_hbm, down_ref, sems):
    group = lax.axis_index("hid") // MDL
    count = down_ref.shape[0]

    def copy(c):
        return pltpu.make_async_copy(down_hbm.at[0, list_ref[group, c]], down_ref.at[c], sems.at[c])

    @pl.loop(0, count)
    def _(c):
        copy(c).start()

    @pl.loop(0, count)
    def _(c):
        copy(c).wait()


def fetch_down(block_list, down_w):
    count = block_list.shape[1]
    unit, depth = down_w.shape[2:]
    return pl.pallas_call(
        fetch_down_kernel,
        out_shape=jax.ShapeDtypeStruct((count, unit, depth), jnp.bfloat16),
        in_specs=[SMEM, ANY],
        out_specs=VMEM,
        scratch_shapes=[pltpu.SemaphoreType.DMA((count,))],
        compiler_params=pltpu.CompilerParams(vmem_limit_bytes=12 * 2**20),
        cost_estimate=pl.CostEstimate(flops=0, bytes_accessed=2 * count * depth * unit * 2, transcendentals=0),
        name="fetch_down",
    )(block_list, down_w)


def gate_up_kernel(x_ref, both_ref, keep_ref, sent_ref):
    upper = lax.axis_index("hid") % 2
    rows = x_ref.shape[0]
    half = rows // 2
    count, _, twice = both_ref.shape
    unit = twice // 2
    kept = x_ref[pl.ds(pl.multiple_of(upper * half, half), half), :]
    other = x_ref[pl.ds(pl.multiple_of((1 - upper) * half, half), half), :]
    x = jnp.concatenate([kept, other], axis=0)
    for c in range(count):
        pair = jnp.dot(x, both_ref[c], preferred_element_type=jnp.float32)
        for k in range(2):
            part = pair[:, k * unit : (k + 1) * unit]
            at = pl.ds((k * count + c) * unit, unit)
            keep_ref[:, at] = part[:half]
            sent_ref[:, at] = part[half:].astype(jnp.bfloat16)


def gate_up(x, both):
    rows = x.shape[0]
    count, depth, twice = both.shape
    return pl.pallas_call(
        gate_up_kernel,
        out_shape=(
            jax.ShapeDtypeStruct((rows // 2, count * twice), jnp.float32),
            jax.ShapeDtypeStruct((rows // 2, count * twice), jnp.bfloat16),
        ),
        in_specs=[VMEM, VMEM],
        out_specs=(VMEM, VMEM),
        compiler_params=pltpu.CompilerParams(vmem_limit_bytes=30 * 2**20),
        name="gate_up",
    )(x, both)


def down_kernel(h_ref, w_ref, out_ref):
    count, unit, depth = w_ref.shape
    rows = h_ref.shape[0]
    step = min(512, depth)
    for n in range(depth // step):
        at = pl.ds(n * step, step)
        w = w_ref[:, :, at].reshape(count * unit, step)
        total = jnp.dot(h_ref[...], w, preferred_element_type=jnp.float32)
        out_ref[:, at] = total.astype(jnp.bfloat16)


def down(hidden, weights):
    return pl.pallas_call(
        down_kernel,
        out_shape=jax.ShapeDtypeStruct((hidden.shape[0], weights.shape[2]), jnp.bfloat16),
        in_specs=[VMEM, VMEM],
        out_specs=VMEM,
        compiler_params=pltpu.CompilerParams(vmem_limit_bytes=20 * 2**20),
        name="down",
    )(hidden, weights)


def finish_kernel(mixed_ref, back_ref, out_ref):
    step = back_ref.shape[2]
    for m in range(MDL):
        total = mixed_ref[:, m * step : (m + 1) * step]
        for g in range(back_ref.shape[0] // MDL):
            total = total + back_ref[g * MDL + m].astype(jnp.float32)
        out_ref[:, m * step : (m + 1) * step] = total.astype(jnp.bfloat16)


def finish(mixed, back):
    return pl.pallas_call(
        finish_kernel,
        out_shape=jax.ShapeDtypeStruct(mixed.shape, jnp.bfloat16),
        in_specs=[VMEM, VMEM],
        out_specs=VMEM,
        compiler_params=pltpu.CompilerParams(vmem_limit_bytes=16 * 2**20),
        name="finish",
    )(mixed, back)


def on_device(
    queries,
    k_cache,
    v_cache,
    lengths,
    residual_in,
    norm_gain,
    gate_w,
    up_w,
    down_w,
    block_list,
    block_count,
):
    dev_count = lax.axis_size("hid")
    position = lax.axis_index("hid")
    group_id = position // MDL
    member = position % MDL
    rows_dev = queries.shape[0]
    model_width = residual_in.shape[1]
    slice_width = model_width // MDL
    all_rows = rows_dev * dev_count
    unit = gate_w.shape[3]
    units = block_list.shape[1] * unit

    mixed_rows, send_tiles = attend(
        queries, k_cache, v_cache, lengths, residual_in, norm_gain, dev_count
    )
    arrived = lax.all_to_all(send_tiles, "hid", split_axis=0, concat_axis=0, tiled=True).reshape(
        all_rows, slice_width
    )
    both = fetch_in(block_list, gate_w, up_w)
    part, sent = gate_up(arrived, both)
    part = part + from_partner(sent, 0).astype(jnp.float32)
    half_rows = all_rows // 2
    for bit_num in (1, 2):
        half_rows = half_rows // 2
        upper_half = member // (1 << bit_num) % 2
        sent = lax.dynamic_slice_in_dim(part, (1 - upper_half) * half_rows, half_rows, 0)
        other = from_partner(sent.astype(jnp.bfloat16), bit_num)
        part = lax.dynamic_slice_in_dim(part, upper_half * half_rows, half_rows, 0)
        part = part + other.astype(jnp.float32)
    live_count = lax.dynamic_index_in_dim(block_count, group_id, 0, keepdims=False)
    active = lax.broadcasted_iota(jnp.int32, (1, units), 1) < live_count * unit
    hidden = jnp.where(
        active, jnp.maximum(part[:, :units], 0.0) * part[:, units:], 0.0
    ).astype(jnp.bfloat16)
    for bit_num in (2, 1, 0):
        upper_half = member // (1 << bit_num) % 2
        other = from_partner(hidden, bit_num)
        hidden = jnp.where(
            upper_half == 0,
            jnp.concatenate([hidden, other], axis=0),
            jnp.concatenate([other, hidden], axis=0),
        )
    ffn_part = down(hidden, fetch_down(block_list, down_w))
    returned = lax.all_to_all(
        ffn_part.reshape(dev_count, rows_dev, slice_width),
        "hid",
        split_axis=0,
        concat_axis=0,
        tiled=True,
    )
    return finish(mixed_rows, returned)


def solution(mesh):
    in_specs = (
        P(("groups", "hid"), None, None),
        P(("groups", "hid"), None, None),
        P(("groups", "hid"), None, None),
        P(("groups", "hid")),
        P(("groups", "hid"), None),
        P(),
        P("hid", None, None, None),
        P("hid", None, None, None),
        P("hid", None, None, None),
        P("groups", None),
        P("groups"),
    )
    out_specs = P(("groups", "hid"), None)
    return jax.shard_map(
        on_device, mesh=mesh, in_specs=in_specs, out_specs=out_specs, check_vma=False
    )
```

```python
import functools
import math

import jax
import jax.numpy as jnp
from jax import lax
from jax.experimental import pallas as pl
from jax.experimental.pallas import tpu as pltpu
from jax.sharding import PartitionSpec as P

MDL = 8
VMEM = pl.BlockSpec(memory_space=pltpu.VMEM)
HBM = pl.BlockSpec(memory_space=pltpu.HBM)
ANY = pl.BlockSpec(memory_space=pl.ANY)


CORES = 2
CHIPS = MDL // CORES


def from_partner(value, mask):
    pairs = [(source, source ^ mask) for source in range(lax.axis_size("hid"))]
    return lax.ppermute(value, "hid", pairs)


def place():
    at = lax.axis_index("hid")
    return at // MDL, at // CORES % CHIPS, at % CORES


def in_hbm(value):
    return pltpu.with_memory_space_constraint(value, pltpu.HBM)


def attend_kernel(
    kv_count,
    len_hbm,
    q_hbm,
    k_hbm,
    v_hbm,
    res_hbm,
    gain_hbm,
    mixed_ref,
    kept_ref,
    sent_ref,
    len_ref,
    q_ref,
    k_buf,
    v_buf,
    res_ref,
    gain_ref,
    sems,
):
    rows, heads, size = q_ref.shape
    slots = k_buf.shape[1]
    width = kv_count * size
    per_kv = heads // kv_count
    lines = heads * rows
    pairs = [
        (len_hbm, len_ref),
        (q_hbm, q_ref),
        (k_hbm, k_buf),
        (v_hbm, v_buf),
        (res_hbm, res_ref),
        (gain_hbm, gain_ref),
    ]
    copies = [pltpu.make_async_copy(s, d, sems.at[i]) for i, (s, d) in enumerate(pairs)]
    for copy in copies:
        copy.start()
    line = lax.broadcasted_iota(jnp.int32, (lines, lines), 0)
    taken = lax.broadcasted_iota(jnp.int32, (lines, lines), 1)
    swap = (taken == line % rows * heads + line // rows).astype(jnp.float32).astype(jnp.bfloat16)
    own = (
        lax.broadcasted_iota(jnp.int32, (lines, width), 0) // (per_kv * rows)
        == lax.broadcasted_iota(jnp.int32, (lines, width), 1) // size
    )
    copies[0].wait()
    request = lax.broadcasted_iota(jnp.int32, (lines, 1), 0) % rows
    first = request * slots
    stop = first
    for r in range(rows):
        stop = jnp.where(request == r, r * slots + len_ref[r], stop)
    slot = lax.broadcasted_iota(jnp.int32, (lines, rows * slots), 1)
    valid = (slot >= first) & (slot < stop)
    copies[1].wait()
    q = jnp.dot(
        swap, q_ref[...].reshape(lines, size), preferred_element_type=jnp.float32
    ).astype(jnp.bfloat16)
    wide = jnp.where(own, jnp.concatenate([q] * kv_count, axis=1), jnp.zeros((), jnp.bfloat16))
    copies[2].wait()
    scores = lax.dot_general(
        wide,
        k_buf[...].reshape(rows * slots, width),
        (((1,), (1,)), ((), ())),
        preferred_element_type=jnp.float32,
    ) * (1.0 / math.sqrt(size))
    scores = jnp.where(valid, scores, -1e30)
    top = jnp.max(scores, axis=1, keepdims=True)
    terms = jnp.where(valid, jnp.exp(scores - top), 0.0)
    probs = (terms / jnp.sum(terms, axis=1, keepdims=True)).astype(jnp.bfloat16)
    copies[3].wait()
    values = v_buf[...].reshape(rows * slots, width)
    for j in range(kv_count):
        span = per_kv * rows
        piece = jnp.dot(
            probs[j * span : (j + 1) * span],
            values[:, j * size : (j + 1) * size],
            preferred_element_type=jnp.float32,
        )
        for i in range(per_kv):
            h = j * per_kv + i
            mixed_ref[:, h * size : (h + 1) * size] = piece[i * rows : (i + 1) * rows]
    copies[4].wait()
    copies[5].wait()
    mixed = mixed_ref[...] + res_ref[...].astype(jnp.float32)
    mixed_ref[...] = mixed
    mean_sq = jnp.mean(mixed * mixed, axis=1, keepdims=True)
    normed = (mixed * lax.rsqrt(mean_sq + 1e-05) * gain_ref[...]).astype(jnp.bfloat16)
    _, chip, core = place()
    step = kept_ref.shape[2]
    for q in range(CHIPS):
        first = normed[:, 2 * q * step : (2 * q + 1) * step]
        second = normed[:, (2 * q + 1) * step : (2 * q + 2) * step]
        kept_ref[q ^ chip] = jnp.where(core == 0, first, second)
        sent_ref[q ^ chip] = jnp.where(core == 0, second, first)


def attend(queries, k_cache, v_cache, lengths, residual_in, norm_gain):
    rows, heads, size = queries.shape
    slots, width = k_cache.shape[1:]
    model = residual_in.shape[1]
    return pl.pallas_call(
        functools.partial(attend_kernel, width // size),
        out_shape=(
            pltpu.VMEM((rows, model), jnp.float32),
            pltpu.VMEM((CHIPS, rows, model // MDL), jnp.bfloat16),
            pltpu.VMEM((CHIPS, rows, model // MDL), jnp.bfloat16),
        ),
        in_specs=[HBM] * 6,
        out_specs=(VMEM,) * 3,
        scratch_shapes=[
            pltpu.SMEM((rows,), jnp.int32),
            pltpu.VMEM((rows, heads, size), jnp.bfloat16),
            pltpu.VMEM((rows, slots, width), jnp.bfloat16),
            pltpu.VMEM((rows, slots, width), jnp.bfloat16),
            pltpu.VMEM((rows, model), jnp.bfloat16),
            pltpu.VMEM((1, model), jnp.float32),
            pltpu.SemaphoreType.DMA((6,)),
        ],
        compiler_params=pltpu.CompilerParams(vmem_limit_bytes=20 * 2**20),
        name="attend",
    )(
        *(
            in_hbm(value)
            for value in (
                lengths,
                queries,
                k_cache,
                v_cache,
                residual_in,
                norm_gain.reshape(1, model),
            )
        )
    )


def fetch_kernel(list_hbm, count_hbm, w_hbm, _, out_ref, __, list_ref, count_ref, sems):
    copies = [
        pltpu.make_async_copy(list_hbm, list_ref, sems.at[0]),
        pltpu.make_async_copy(count_hbm, count_ref, sems.at[1]),
    ]
    for copy in copies:
        copy.start()
    for copy in copies:
        copy.wait()
    group, _, _ = place()
    live = count_ref[group]

    def fetched(c):
        return pltpu.make_async_copy(w_hbm.at[0, list_ref[group, c]], out_ref.at[c], sems.at[c])

    @pl.loop(0, live)
    def _(c):
        fetched(c).start()

    @pl.loop(live, out_ref.shape[0])
    def _(c):
        out_ref[c] = jnp.zeros(out_ref.shape[1:], out_ref.dtype)

    @pl.loop(0, live)
    def _(c):
        fetched(c).wait()


def fetch(block_list, block_count, weights, held, name):
    count = block_list.shape[1]
    size = math.prod(weights.shape[2:])
    return pl.pallas_call(
        fetch_kernel,
        out_shape=(
            pltpu.VMEM((count,) + weights.shape[2:], jnp.bfloat16),
            jax.ShapeDtypeStruct(held.shape, held.dtype),
        ),
        in_specs=[HBM] * 3 + [ANY],
        out_specs=(VMEM, ANY),
        input_output_aliases={3: 1},
        scratch_shapes=[
            pltpu.SMEM(block_list.shape, jnp.int32),
            pltpu.SMEM(block_count.shape, jnp.int32),
            pltpu.SemaphoreType.DMA((count,)),
        ],
        compiler_params=pltpu.CompilerParams(vmem_limit_bytes=10 * 2**20),
        cost_estimate=pl.CostEstimate(flops=0, bytes_accessed=4 * count * size, transcendentals=0),
        name=name,
    )(in_hbm(block_list), in_hbm(block_count), in_hbm(weights), held)


def gate_up_kernel(arrived_ref, gate_ref, up_ref, keep_ref, sent_ref, x_ref):
    groups, _, _, rows, _ = arrived_ref.shape
    half = keep_ref.shape[0]
    count, _, unit = gate_ref.shape
    for core in range(CORES):
        for chip in range(CHIPS):
            for group in range(groups):
                at = ((core * CHIPS + chip) * groups + group) * rows
                x_ref[at : at + rows, :] = arrived_ref[group, chip, core].astype(jnp.float32)
    x = x_ref[...].astype(jnp.bfloat16)
    for c in range(count):
        both = jnp.concatenate([gate_ref[c], up_ref[c]], axis=1)
        pair = jnp.dot(x, both, preferred_element_type=jnp.float32)
        for k in range(2):
            part = pair[:, k * unit : (k + 1) * unit]
            at = pl.ds((k * count + c) * unit, unit)
            keep_ref[:, at] = part[:half]
            sent_ref[:, at] = part[half:].astype(jnp.bfloat16)


def gate_up(arrived, gate, up):
    rows = math.prod(arrived.shape[:4])
    count, depth, unit = gate.shape
    return pl.pallas_call(
        gate_up_kernel,
        out_shape=(
            pltpu.VMEM((rows // 2, 2 * count * unit), jnp.float32),
            pltpu.VMEM((rows // 2, 2 * count * unit), jnp.bfloat16),
        ),
        in_specs=[VMEM] * 3,
        out_specs=(VMEM, VMEM),
        scratch_shapes=[pltpu.VMEM((rows, depth), jnp.float32)],
        compiler_params=pltpu.CompilerParams(vmem_limit_bytes=24 * 2**20),
        name="gate_up",
    )(arrived, gate, up)


def down_kernel(near_ref, far_ref, w_ref, out_ref):
    count, unit, depth = w_ref.shape
    devices, rows, _ = out_ref.shape
    groups = devices // MDL
    group, chip, core = place()
    hidden = jnp.concatenate([near_ref[...], far_ref[...]], axis=0)
    step = min(512, depth)
    for n in range(depth // step):
        at = pl.ds(n * step, step)
        w = w_ref[:, :, at].reshape(count * unit, step)
        total = jnp.dot(hidden, w, preferred_element_type=jnp.float32)
        for r in range(devices):
            c, q, g = r // (CHIPS * groups), r // groups % CHIPS, r % groups
            owner = (group ^ g) * MDL + (chip ^ q) * CORES + (core ^ c)
            out_ref[owner, :, at] = total[r * rows : (r + 1) * rows].astype(jnp.bfloat16)


def down(near, far, weights, devices):
    rows = 2 * near.shape[0] // devices
    return pl.pallas_call(
        down_kernel,
        out_shape=pltpu.VMEM((devices, rows, weights.shape[2]), jnp.bfloat16),
        in_specs=[VMEM] * 3,
        out_specs=VMEM,
        compiler_params=pltpu.CompilerParams(vmem_limit_bytes=20 * 2**20),
        name="down",
    )(near, far, weights)


def finish_kernel(mixed_ref, back_ref, out_ref):
    step = back_ref.shape[2]
    for m in range(MDL):
        total = mixed_ref[:, m * step : (m + 1) * step]
        for g in range(back_ref.shape[0] // MDL):
            total = total + back_ref[g * MDL + m].astype(jnp.float32)
        out_ref[:, m * step : (m + 1) * step] = total.astype(jnp.bfloat16)


def finish(mixed, back):
    return pl.pallas_call(
        finish_kernel,
        out_shape=jax.ShapeDtypeStruct(mixed.shape, jnp.bfloat16),
        in_specs=[VMEM, VMEM],
        out_specs=VMEM,
        compiler_params=pltpu.CompilerParams(vmem_limit_bytes=16 * 2**20),
        name="finish",
    )(mixed, back)


def on_device(
    queries,
    k_cache,
    v_cache,
    lengths,
    residual_in,
    norm_gain,
    gate_w,
    up_w,
    down_w,
    block_list,
    block_count,
):
    dev_count = lax.axis_size("hid")
    group_total = dev_count // MDL
    rows_dev = queries.shape[0]
    units = block_list.shape[1] * gate_w.shape[3]
    masks = [chip * CORES for chip in range(CHIPS)]
    far_first = range(CHIPS - 1, 0, -1)

    mixed_rows, kept, sent = attend(queries, k_cache, v_cache, lengths, residual_in, norm_gain)
    pair = jnp.stack([kept, from_partner(sent, 1)], axis=1)
    came = {chip: from_partner(pair[chip], masks[chip]) for chip in far_first}
    gate, own = fetch(block_list, block_count, gate_w, pair[0], "fetch_gate")
    arrived = jnp.stack([own] + [came[chip] for chip in range(1, CHIPS)])[None]
    came = from_partner(arrived, MDL)
    up, arrived = fetch(block_list, block_count, up_w, arrived, "fetch_up")
    arrived = jnp.concatenate([arrived, came], axis=0)
    for level in range(1, group_total.bit_length() - 1):
        arrived = jnp.concatenate([arrived, from_partner(arrived, MDL << level)], axis=0)

    part, sent = gate_up(arrived, gate, up)
    part = part + from_partner(sent, 1).astype(jnp.float32)
    part = part.reshape(CHIPS, group_total * rows_dev, 2 * units)
    came = [from_partner(part[chip].astype(jnp.bfloat16), masks[chip]) for chip in far_first]
    down_rows, total = fetch(block_list, block_count, down_w, part[0], "fetch_down")
    for piece in came:
        total = total + piece.astype(jnp.float32)
    hidden = (jnp.maximum(total[:, :units], 0.0) * total[:, units:]).astype(jnp.bfloat16)

    came = {chip: from_partner(hidden, masks[chip]) for chip in far_first}
    near = jnp.concatenate([hidden] + [came[chip] for chip in range(1, CHIPS)], axis=0)
    far = from_partner(near, 1)
    ffn_part = down(near, far, down_rows, dev_count)
    returned = lax.all_to_all(ffn_part, "hid", split_axis=0, concat_axis=0, tiled=True)
    return finish(mixed_rows, returned)


def solution(mesh):
    in_specs = (
        P(("groups", "hid"), None, None),
        P(("groups", "hid"), None, None),
        P(("groups", "hid"), None, None),
        P(("groups", "hid")),
        P(("groups", "hid"), None),
        P(),
        P("hid", None, None, None),
        P("hid", None, None, None),
        P("hid", None, None, None),
        P("groups", None),
        P("groups"),
    )
    out_specs = P(("groups", "hid"), None)
    return jax.shard_map(
        on_device, mesh=mesh, in_specs=in_specs, out_specs=out_specs, check_vma=False
    )
```

```python
import functools
import math

import jax
import jax.numpy as jnp
from jax import lax
from jax.experimental import pallas as pl
from jax.experimental.pallas import tpu as pltpu
from jax.sharding import PartitionSpec as P

MDL = 8
VMEM = pl.BlockSpec(memory_space=pltpu.VMEM)
HBM = pl.BlockSpec(memory_space=pltpu.HBM)
ANY = pl.BlockSpec(memory_space=pl.ANY)


CORES = 2
CHIPS = MDL // CORES


def from_partner(value, mask):
    pairs = [(source, source ^ mask) for source in range(lax.axis_size("hid"))]
    return lax.ppermute(value, "hid", pairs)


def place():
    at = lax.axis_index("hid")
    return at // MDL, at // CORES % CHIPS, at % CORES


def in_hbm(value):
    return pltpu.with_memory_space_constraint(value, pltpu.HBM)


def block_copy(list_ref, w_hbm, out_ref, sems, c):
    group, _, _ = place()
    return pltpu.make_async_copy(w_hbm.at[0, list_ref[group, c]], out_ref.at[c], sems.at[c])


def start_blocks(list_ref, count_ref, w_hbm, out_ref, sems):
    live = count_ref[place()[0]]

    @pl.loop(0, live)
    def _(c):
        block_copy(list_ref, w_hbm, out_ref, sems, c).start()

    @pl.loop(live, out_ref.shape[0])
    def _(c):
        out_ref[c] = jnp.zeros(out_ref.shape[1:], out_ref.dtype)


def wait_blocks(list_ref, count_ref, w_hbm, out_ref, sems):
    @pl.loop(0, count_ref[place()[0]])
    def _(c):
        block_copy(list_ref, w_hbm, out_ref, sems, c).wait()


def attend_kernel(
    kv_count,
    len_hbm,
    q_hbm,
    k_hbm,
    v_hbm,
    res_hbm,
    gain_hbm,
    list_hbm,
    count_hbm,
    gate_hbm,
    mixed_ref,
    kept_ref,
    sent_ref,
    gate_ref,
    len_ref,
    q_ref,
    k_buf,
    v_buf,
    res_ref,
    gain_ref,
    list_ref,
    count_ref,
    sems,
    block_sems,
):
    rows, heads, size = q_ref.shape
    slots = k_buf.shape[1]
    width = kv_count * size
    per_kv = heads // kv_count
    lines = heads * rows
    pairs = [
        (len_hbm, len_ref),
        (q_hbm, q_ref),
        (k_hbm, k_buf),
        (v_hbm, v_buf),
        (res_hbm, res_ref),
        (gain_hbm, gain_ref),
        (list_hbm, list_ref),
        (count_hbm, count_ref),
    ]
    copies = [pltpu.make_async_copy(s, d, sems.at[i]) for i, (s, d) in enumerate(pairs)]
    for copy in copies[6:] + copies[:6]:
        copy.start()
    copies[6].wait()
    copies[7].wait()
    start_blocks(list_ref, count_ref, gate_hbm, gate_ref, block_sems)
    line = lax.broadcasted_iota(jnp.int32, (lines, lines), 0)
    taken = lax.broadcasted_iota(jnp.int32, (lines, lines), 1)
    swap = (taken == line % rows * heads + line // rows).astype(jnp.float32).astype(jnp.bfloat16)
    own = (
        lax.broadcasted_iota(jnp.int32, (lines, width), 0) // (per_kv * rows)
        == lax.broadcasted_iota(jnp.int32, (lines, width), 1) // size
    )
    copies[0].wait()
    request = lax.broadcasted_iota(jnp.int32, (lines, 1), 0) % rows
    first = request * slots
    stop = first
    for r in range(rows):
        stop = jnp.where(request == r, r * slots + len_ref[r], stop)
    slot = lax.broadcasted_iota(jnp.int32, (lines, rows * slots), 1)
    valid = (slot >= first) & (slot < stop)
    copies[1].wait()
    q = jnp.dot(
        swap, q_ref[...].reshape(lines, size), preferred_element_type=jnp.float32
    ).astype(jnp.bfloat16)
    wide = jnp.where(own, jnp.concatenate([q] * kv_count, axis=1), jnp.zeros((), jnp.bfloat16))
    copies[2].wait()
    scores = lax.dot_general(
        wide,
        k_buf[...].reshape(rows * slots, width),
        (((1,), (1,)), ((), ())),
        preferred_element_type=jnp.float32,
    ) * (1.0 / math.sqrt(size))
    scores = jnp.where(valid, scores, -1e30)
    top = jnp.max(scores, axis=1, keepdims=True)
    terms = jnp.where(valid, jnp.exp(scores - top), 0.0)
    probs = (terms / jnp.sum(terms, axis=1, keepdims=True)).astype(jnp.bfloat16)
    copies[3].wait()
    values = v_buf[...].reshape(rows * slots, width)
    for j in range(kv_count):
        span = per_kv * rows
        piece = jnp.dot(
            probs[j * span : (j + 1) * span],
            values[:, j * size : (j + 1) * size],
            preferred_element_type=jnp.float32,
        )
        for i in range(per_kv):
            h = j * per_kv + i
            mixed_ref[:, h * size : (h + 1) * size] = piece[i * rows : (i + 1) * rows]
    copies[4].wait()
    copies[5].wait()
    mixed = mixed_ref[...] + res_ref[...].astype(jnp.float32)
    mixed_ref[...] = mixed
    mean_sq = jnp.mean(mixed * mixed, axis=1, keepdims=True)
    normed = (mixed * lax.rsqrt(mean_sq + 1e-05) * gain_ref[...]).astype(jnp.bfloat16)
    _, chip, core = place()
    step = kept_ref.shape[2]
    for q in range(CHIPS):
        first = normed[:, 2 * q * step : (2 * q + 1) * step]
        second = normed[:, (2 * q + 1) * step : (2 * q + 2) * step]
        kept_ref[q ^ chip] = jnp.where(core == 0, first, second)
        sent_ref[q ^ chip] = jnp.where(core == 0, second, first)
    wait_blocks(list_ref, count_ref, gate_hbm, gate_ref, block_sems)


def attend(
    queries, k_cache, v_cache, lengths, residual_in, norm_gain, block_list, block_count, gate_w
):
    rows, heads, size = queries.shape
    slots, width = k_cache.shape[1:]
    model = residual_in.shape[1]
    return pl.pallas_call(
        functools.partial(attend_kernel, width // size),
        out_shape=(
            pltpu.VMEM((rows, model), jnp.float32),
            pltpu.VMEM((CHIPS, rows, model // MDL), jnp.bfloat16),
            pltpu.VMEM((CHIPS, rows, model // MDL), jnp.bfloat16),
            pltpu.VMEM(block_list.shape[1:] + gate_w.shape[2:], jnp.bfloat16),
        ),
        in_specs=[HBM] * 9,
        out_specs=(VMEM,) * 4,
        scratch_shapes=[
            pltpu.SMEM((rows,), jnp.int32),
            pltpu.VMEM((rows, heads, size), jnp.bfloat16),
            pltpu.VMEM((rows, slots, width), jnp.bfloat16),
            pltpu.VMEM((rows, slots, width), jnp.bfloat16),
            pltpu.VMEM((rows, model), jnp.bfloat16),
            pltpu.VMEM((1, model), jnp.float32),
            pltpu.SMEM(block_list.shape, jnp.int32),
            pltpu.SMEM(block_count.shape, jnp.int32),
            pltpu.SemaphoreType.DMA((8,)),
            pltpu.SemaphoreType.DMA(block_list.shape[1:]),
        ],
        compiler_params=pltpu.CompilerParams(vmem_limit_bytes=20 * 2**20),
        name="attend",
    )(
        *(
            in_hbm(value)
            for value in (
                lengths,
                queries,
                k_cache,
                v_cache,
                residual_in,
                norm_gain.reshape(1, model),
                block_list,
                block_count,
                gate_w,
            )
        )
    )


def fetch_kernel(list_hbm, count_hbm, w_hbm, _, out_ref, *rest):
    list_ref, count_ref, sems, block_sems = rest[-4:]
    copies = [
        pltpu.make_async_copy(list_hbm, list_ref, sems.at[0]),
        pltpu.make_async_copy(count_hbm, count_ref, sems.at[1]),
    ]
    for copy in copies:
        copy.start()
    for copy in copies:
        copy.wait()
    start_blocks(list_ref, count_ref, w_hbm, out_ref, block_sems)
    wait_blocks(list_ref, count_ref, w_hbm, out_ref, block_sems)


def fetch(block_list, block_count, weights, held, name, passed=True):
    count = block_list.shape[1]
    size = math.prod(weights.shape[2:])
    blocks = pltpu.VMEM((count,) + weights.shape[2:], jnp.bfloat16)
    return pl.pallas_call(
        fetch_kernel,
        out_shape=(blocks, jax.ShapeDtypeStruct(held.shape, held.dtype)) if passed else blocks,
        in_specs=[HBM] * 3 + [ANY],
        out_specs=(VMEM, ANY) if passed else VMEM,
        input_output_aliases={3: 1} if passed else {},
        scratch_shapes=[
            pltpu.SMEM(block_list.shape, jnp.int32),
            pltpu.SMEM(block_count.shape, jnp.int32),
            pltpu.SemaphoreType.DMA((2,)),
            pltpu.SemaphoreType.DMA((count,)),
        ],
        compiler_params=pltpu.CompilerParams(vmem_limit_bytes=10 * 2**20),
        cost_estimate=pl.CostEstimate(flops=0, bytes_accessed=4 * count * size, transcendentals=0),
        name=name,
    )(in_hbm(block_list), in_hbm(block_count), in_hbm(weights), held)


def gate_up_kernel(arrived_ref, gate_ref, up_ref, keep_ref, sent_ref, x_ref):
    groups, _, _, rows, _ = arrived_ref.shape
    half = keep_ref.shape[0]
    count, _, unit = gate_ref.shape
    for core in range(CORES):
        for chip in range(CHIPS):
            for group in range(groups):
                at = ((core * CHIPS + chip) * groups + group) * rows
                x_ref[at : at + rows, :] = arrived_ref[group, chip, core].astype(jnp.float32)
    x = x_ref[...].astype(jnp.bfloat16)
    for c in range(count):
        both = jnp.concatenate([gate_ref[c], up_ref[c]], axis=1)
        pair = jnp.dot(x, both, preferred_element_type=jnp.float32)
        for k in range(2):
            part = pair[:, k * unit : (k + 1) * unit]
            at = pl.ds((k * count + c) * unit, unit)
            keep_ref[:, at] = part[:half]
            sent_ref[:, at] = part[half:].astype(jnp.bfloat16)


def gate_up(arrived, gate, up):
    rows = math.prod(arrived.shape[:4])
    count, depth, unit = gate.shape
    return pl.pallas_call(
        gate_up_kernel,
        out_shape=(
            pltpu.VMEM((rows // 2, 2 * count * unit), jnp.float32),
            pltpu.VMEM((rows // 2, 2 * count * unit), jnp.bfloat16),
        ),
        in_specs=[VMEM] * 3,
        out_specs=(VMEM, VMEM),
        scratch_shapes=[pltpu.VMEM((rows, depth), jnp.float32)],
        compiler_params=pltpu.CompilerParams(vmem_limit_bytes=24 * 2**20),
        name="gate_up",
    )(arrived, gate, up)


def down_kernel(near_ref, far_ref, w_ref, out_ref):
    count, unit, depth = w_ref.shape
    devices, rows, _ = out_ref.shape
    groups = devices // MDL
    group, chip, core = place()
    hidden = jnp.concatenate([near_ref[...], far_ref[...]], axis=0)
    step = min(512, depth)
    for n in range(depth // step):
        at = pl.ds(n * step, step)
        w = w_ref[:, :, at].reshape(count * unit, step)
        total = jnp.dot(hidden, w, preferred_element_type=jnp.float32)
        for r in range(devices):
            c, q, g = r // (CHIPS * groups), r // groups % CHIPS, r % groups
            owner = (group ^ g) * MDL + (chip ^ q) * CORES + (core ^ c)
            out_ref[owner, :, at] = total[r * rows : (r + 1) * rows].astype(jnp.bfloat16)


def down(near, far, weights, devices):
    rows = 2 * near.shape[0] // devices
    return pl.pallas_call(
        down_kernel,
        out_shape=pltpu.VMEM((devices, rows, weights.shape[2]), jnp.bfloat16),
        in_specs=[VMEM] * 3,
        out_specs=VMEM,
        compiler_params=pltpu.CompilerParams(vmem_limit_bytes=20 * 2**20),
        name="down",
    )(near, far, weights)


def finish_kernel(mixed_ref, back_ref, out_ref):
    step = back_ref.shape[2]
    for m in range(MDL):
        total = mixed_ref[:, m * step : (m + 1) * step]
        for g in range(back_ref.shape[0] // MDL):
            total = total + back_ref[g * MDL + m].astype(jnp.float32)
        out_ref[:, m * step : (m + 1) * step] = total.astype(jnp.bfloat16)


def finish(mixed, back):
    return pl.pallas_call(
        finish_kernel,
        out_shape=jax.ShapeDtypeStruct(mixed.shape, jnp.bfloat16),
        in_specs=[VMEM, VMEM],
        out_specs=VMEM,
        compiler_params=pltpu.CompilerParams(vmem_limit_bytes=16 * 2**20),
        name="finish",
    )(mixed, back)


def on_device(
    queries,
    k_cache,
    v_cache,
    lengths,
    residual_in,
    norm_gain,
    gate_w,
    up_w,
    down_w,
    block_list,
    block_count,
):
    dev_count = lax.axis_size("hid")
    group_total = dev_count // MDL
    rows_dev = queries.shape[0]
    units = block_list.shape[1] * gate_w.shape[3]
    masks = [chip * CORES for chip in range(CHIPS)]
    far_first = range(CHIPS - 1, 0, -1)

    mixed_rows, kept, sent, gate = attend(
        queries, k_cache, v_cache, lengths, residual_in, norm_gain, block_list, block_count, gate_w
    )
    pair = jnp.stack([kept, from_partner(sent, 1)], axis=1)
    came = {chip: from_partner(pair[chip], masks[chip]) for chip in far_first}
    arrived = jnp.stack([pair[0]] + [came[chip] for chip in range(1, CHIPS)])[None]
    up = fetch(block_list, block_count, up_w, arrived, "fetch_up", passed=False)
    for level in range(group_total.bit_length() - 1):
        arrived = jnp.concatenate([arrived, from_partner(arrived, MDL << level)], axis=0)

    part, sent = gate_up(arrived, gate, up)
    part = part + from_partner(sent, 1).astype(jnp.float32)
    part = part.reshape(CHIPS, group_total * rows_dev, 2 * units)
    came = [from_partner(part[chip].astype(jnp.bfloat16), masks[chip]) for chip in far_first]
    down_rows, total = fetch(block_list, block_count, down_w, part[0], "fetch_down")
    for piece in came:
        total = total + piece.astype(jnp.float32)
    hidden = (jnp.maximum(total[:, :units], 0.0) * total[:, units:]).astype(jnp.bfloat16)

    came = {chip: from_partner(hidden, masks[chip]) for chip in far_first}
    near = jnp.concatenate([hidden] + [came[chip] for chip in range(1, CHIPS)], axis=0)
    far = from_partner(near, 1)
    ffn_part = down(near, far, down_rows, dev_count)
    returned = lax.all_to_all(ffn_part, "hid", split_axis=0, concat_axis=0, tiled=True)
    return finish(mixed_rows, returned)


def solution(mesh):
    in_specs = (
        P(("groups", "hid"), None, None),
        P(("groups", "hid"), None, None),
        P(("groups", "hid"), None, None),
        P(("groups", "hid")),
        P(("groups", "hid"), None),
        P(),
        P("hid", None, None, None),
        P("hid", None, None, None),
        P("hid", None, None, None),
        P("groups", None),
        P("groups"),
    )
    out_specs = P(("groups", "hid"), None)
    return jax.shard_map(
        on_device, mesh=mesh, in_specs=in_specs, out_specs=out_specs, check_vma=False
    )
```

```python
import functools
import math

import jax
import jax.numpy as jnp
from jax import lax
from jax.experimental import pallas as pl
from jax.experimental.pallas import tpu as pltpu
from jax.sharding import PartitionSpec as P

MDL = 8
VMEM = pl.BlockSpec(memory_space=pltpu.VMEM)
HBM = pl.BlockSpec(memory_space=pltpu.HBM)
ANY = pl.BlockSpec(memory_space=pl.ANY)


CORES = 2
CHIPS = MDL // CORES


def from_partner(value, mask):
    pairs = [(source, source ^ mask) for source in range(lax.axis_size("hid"))]
    return lax.ppermute(value, "hid", pairs)


def place():
    at = lax.axis_index("hid")
    return at // MDL, at // CORES % CHIPS, at % CORES


def in_hbm(value):
    return pltpu.with_memory_space_constraint(value, pltpu.HBM)


def block_copies(listed, w_hbm, out_ref, sems):
    return [
        pltpu.make_async_copy(w_hbm.at[0, block], out_ref.at[c], sems.at[c]) for c, block in enumerate(listed)
    ]


def attend_kernel(
    kv_count,
    len_hbm,
    q_hbm,
    k_hbm,
    v_hbm,
    res_hbm,
    gain_hbm,
    list_hbm,
    count_hbm,
    gate_hbm,
    mixed_ref,
    kept_ref,
    sent_ref,
    row_ref,
    live_ref,
    gate_ref,
    len_ref,
    q_ref,
    k_buf,
    v_buf,
    res_ref,
    gain_ref,
    list_ref,
    count_ref,
    sems,
    block_sems,
):
    rows, heads, size = q_ref.shape
    slots = k_buf.shape[1]
    width = kv_count * size
    per_kv = heads // kv_count
    lines = heads * rows
    pairs = [
        (len_hbm, len_ref),
        (q_hbm, q_ref),
        (k_hbm, k_buf),
        (v_hbm, v_buf),
        (res_hbm, res_ref),
        (gain_hbm, gain_ref),
        (list_hbm, list_ref),
        (count_hbm, count_ref),
        (list_hbm, row_ref),
    ]
    copies = [pltpu.make_async_copy(s, d, sems.at[i]) for i, (s, d) in enumerate(pairs)]
    for copy in copies[6:] + copies[:6]:
        copy.start()
    copies[6].wait()
    copies[7].wait()
    group, chip, core = place()
    early = [list_ref[group, c] for c in range(gate_ref.shape[0])]
    blocks = block_copies(early, gate_hbm, gate_ref, block_sems)
    for copy in blocks:
        copy.start()
    live_lanes = count_ref[group] * (live_ref.shape[1] // list_ref.shape[1])
    lane = lax.broadcasted_iota(jnp.int32, live_ref.shape, 1)
    live_ref[...] = (lane < live_lanes).astype(jnp.float32)
    line = lax.broadcasted_iota(jnp.int32, (lines, lines), 0)
    taken = lax.broadcasted_iota(jnp.int32, (lines, lines), 1)
    swap = (taken == line % rows * heads + line // rows).astype(jnp.float32).astype(jnp.bfloat16)
    own = (
        lax.broadcasted_iota(jnp.int32, (lines, width), 0) // (per_kv * rows)
        == lax.broadcasted_iota(jnp.int32, (lines, width), 1) // size
    )
    copies[0].wait()
    request = lax.broadcasted_iota(jnp.int32, (lines, 1), 0) % rows
    first = request * slots
    stop = first
    for r in range(rows):
        stop = jnp.where(request == r, r * slots + len_ref[r], stop)
    slot = lax.broadcasted_iota(jnp.int32, (lines, rows * slots), 1)
    valid = (slot >= first) & (slot < stop)
    copies[1].wait()
    q = jnp.dot(
        swap, q_ref[...].reshape(lines, size), preferred_element_type=jnp.float32
    ).astype(jnp.bfloat16)
    wide = jnp.where(own, jnp.concatenate([q] * kv_count, axis=1), jnp.zeros((), jnp.bfloat16))
    copies[2].wait()
    scores = lax.dot_general(
        wide,
        k_buf[...].reshape(rows * slots, width),
        (((1,), (1,)), ((), ())),
        preferred_element_type=jnp.float32,
    ) * (1.0 / math.sqrt(size))
    scores = jnp.where(valid, scores, -1e30)
    top = jnp.max(scores, axis=1, keepdims=True)
    terms = jnp.where(valid, jnp.exp(scores - top), 0.0)
    probs = (terms / jnp.sum(terms, axis=1, keepdims=True)).astype(jnp.bfloat16)
    copies[3].wait()
    values = v_buf[...].reshape(rows * slots, width)
    for j in range(kv_count):
        span = per_kv * rows
        piece = jnp.dot(
            probs[j * span : (j + 1) * span],
            values[:, j * size : (j + 1) * size],
            preferred_element_type=jnp.float32,
        )
        for i in range(per_kv):
            h = j * per_kv + i
            mixed_ref[:, h * size : (h + 1) * size] = piece[i * rows : (i + 1) * rows]
    copies[4].wait()
    copies[5].wait()
    mixed = mixed_ref[...] + res_ref[...].astype(jnp.float32)
    mixed_ref[...] = mixed
    mean_sq = jnp.mean(mixed * mixed, axis=1, keepdims=True)
    normed = (mixed * lax.rsqrt(mean_sq + 1e-05) * gain_ref[...]).astype(jnp.bfloat16)
    step = kept_ref.shape[2]
    for q in range(CHIPS):
        first = normed[:, 2 * q * step : (2 * q + 1) * step]
        second = normed[:, (2 * q + 1) * step : (2 * q + 2) * step]
        kept_ref[q ^ chip] = jnp.where(core == 0, first, second)
        sent_ref[q ^ chip] = jnp.where(core == 0, second, first)
    for copy in blocks + copies[8:]:
        copy.wait()


def attend(
    queries, k_cache, v_cache, lengths, residual_in, norm_gain, block_list, block_count, gate_w, early
):
    rows, heads, size = queries.shape
    slots, width = k_cache.shape[1:]
    model = residual_in.shape[1]
    return pl.pallas_call(
        functools.partial(attend_kernel, width // size),
        out_shape=(
            pltpu.VMEM((rows, model), jnp.float32),
            pltpu.VMEM((CHIPS, rows, model // MDL), jnp.bfloat16),
            pltpu.VMEM((CHIPS, rows, model // MDL), jnp.bfloat16),
            pltpu.VMEM(block_list.shape, jnp.int32),
            pltpu.VMEM((1, block_list.shape[1] * gate_w.shape[3]), jnp.float32),
            pltpu.VMEM((early,) + gate_w.shape[2:], jnp.bfloat16),
        ),
        in_specs=[HBM] * 9,
        out_specs=(VMEM,) * 6,
        scratch_shapes=[
            pltpu.SMEM((rows,), jnp.int32),
            pltpu.VMEM((rows, heads, size), jnp.bfloat16),
            pltpu.VMEM((rows, slots, width), jnp.bfloat16),
            pltpu.VMEM((rows, slots, width), jnp.bfloat16),
            pltpu.VMEM((rows, model), jnp.bfloat16),
            pltpu.VMEM((1, model), jnp.float32),
            pltpu.SMEM(block_list.shape, jnp.int32),
            pltpu.SMEM(block_count.shape, jnp.int32),
            pltpu.SemaphoreType.DMA((9,)),
            pltpu.SemaphoreType.DMA((early,)),
        ],
        compiler_params=pltpu.CompilerParams(vmem_limit_bytes=20 * 2**20),
        name="attend",
    )(
        *(
            in_hbm(value)
            for value in (
                lengths,
                queries,
                k_cache,
                v_cache,
                residual_in,
                norm_gain.reshape(1, model),
                block_list,
                block_count,
                gate_w,
            )
        )
    )


def fetch_kernel(firsts, rows_ref, *rest):
    parts = len(firsts)
    row = rows_ref[pl.ds(place()[0], 1), :]
    at = lax.broadcasted_iota(jnp.int32, row.shape, 1)
    copies = []
    for i, first in enumerate(firsts):
        out_ref = rest[parts + 1 + i]
        listed = [jnp.sum(jnp.where(at == first + c, row, 0)) for c in range(out_ref.shape[0])]
        copies += block_copies(listed, rest[i], out_ref, rest[-parts + i])
    for copy in copies:
        copy.start()
    for copy in copies:
        copy.wait()


def fetch(rows, parts, held, name, passed):
    out_shape = [pltpu.VMEM((stop - first,) + w.shape[2:], jnp.bfloat16) for w, first, stop in parts]
    size = 2 * sum(math.prod(blocks.shape) for blocks in out_shape)
    out_specs = [VMEM] * len(parts)
    if passed:
        out_shape.append(jax.ShapeDtypeStruct(held.shape, held.dtype))
        out_specs.append(ANY)
    return pl.pallas_call(
        functools.partial(fetch_kernel, [first for _, first, _ in parts]),
        out_shape=out_shape,
        in_specs=[VMEM] + [HBM] * len(parts) + [ANY],
        out_specs=out_specs,
        input_output_aliases={1 + len(parts): len(parts)} if passed else {},
        scratch_shapes=[pltpu.SemaphoreType.DMA((stop - first,)) for _, first, stop in parts],
        compiler_params=pltpu.CompilerParams(vmem_limit_bytes=12 * 2**20),
        cost_estimate=pl.CostEstimate(flops=0, bytes_accessed=2 * size, transcendentals=0),
        name=name,
    )(rows, *(in_hbm(w) for w, _, _ in parts), held)


def gate_up_kernel(arrived_ref, gate_near, gate_far, up_near, up_far, live_ref, keep_ref, sent_ref, x_ref):
    groups, _, _, rows, _ = arrived_ref.shape
    half = keep_ref.shape[0]
    unit = gate_near.shape[2]
    gates = [near_or_far.at[c] for near_or_far in (gate_near, gate_far) for c in range(near_or_far.shape[0])]
    ups = [near_or_far.at[c] for near_or_far in (up_near, up_far) for c in range(near_or_far.shape[0])]
    count = len(gates)
    for core in range(CORES):
        for chip in range(CHIPS):
            for group in range(groups):
                at = ((core * CHIPS + chip) * groups + group) * rows
                x_ref[at : at + rows, :] = arrived_ref[group, chip, core].astype(jnp.float32)
    x = x_ref[...].astype(jnp.bfloat16)
    for c in range(count):
        both = jnp.concatenate([gates[c][...], ups[c][...]], axis=1)
        pair = jnp.dot(x, both, preferred_element_type=jnp.float32)
        for k in range(2):
            part = pair[:, k * unit : (k + 1) * unit]
            if k == 0:
                live = live_ref[:, c * unit : (c + 1) * unit] > 0.0
                part = jnp.where(live, part, 0.0)
            at = pl.ds((k * count + c) * unit, unit)
            keep_ref[:, at] = part[:half]
            sent_ref[:, at] = part[half:].astype(jnp.bfloat16)


def gate_up(arrived, gate, up, live):
    rows = math.prod(arrived.shape[:4])
    _, depth, unit = gate[0].shape
    wide = 2 * unit * sum(part.shape[0] for part in gate)
    return pl.pallas_call(
        gate_up_kernel,
        out_shape=(
            pltpu.VMEM((rows // 2, wide), jnp.float32),
            pltpu.VMEM((rows // 2, wide), jnp.bfloat16),
        ),
        in_specs=[VMEM] * 6,
        out_specs=(VMEM, VMEM),
        scratch_shapes=[pltpu.VMEM((rows, depth), jnp.float32)],
        compiler_params=pltpu.CompilerParams(vmem_limit_bytes=24 * 2**20),
        name="gate_up",
    )(arrived, *gate, *up, live)


def down_kernel(*refs):
    *pieces, w_ref, out_ref = refs
    count, unit, depth = w_ref.shape
    devices, rows, _ = out_ref.shape
    groups = devices // MDL
    group, chip, core = place()
    hidden = jnp.concatenate([piece[...] for piece in pieces], axis=0)
    step = min(512, depth)
    for n in range(depth // step):
        at = pl.ds(n * step, step)
        w = w_ref[:, :, at].reshape(count * unit, step)
        total = jnp.dot(hidden, w, preferred_element_type=jnp.float32)
        for r in range(devices):
            c, q, g = r // (CHIPS * groups), r // groups % CHIPS, r % groups
            owner = (group ^ g) * MDL + (chip ^ q) * CORES + (core ^ c)
            out_ref[owner, :, at] = total[r * rows : (r + 1) * rows].astype(jnp.bfloat16)


def down(pieces, weights, devices):
    rows = sum(piece.shape[0] for piece in pieces) // devices
    return pl.pallas_call(
        down_kernel,
        out_shape=pltpu.VMEM((devices, rows, weights.shape[2]), jnp.bfloat16),
        in_specs=[VMEM] * (len(pieces) + 1),
        out_specs=VMEM,
        compiler_params=pltpu.CompilerParams(vmem_limit_bytes=20 * 2**20),
        name="down",
    )(*pieces, weights)


def finish_kernel(mixed_ref, back_ref, out_ref):
    step = back_ref.shape[2]
    for m in range(MDL):
        total = mixed_ref[:, m * step : (m + 1) * step]
        for g in range(back_ref.shape[0] // MDL):
            total = total + back_ref[g * MDL + m].astype(jnp.float32)
        out_ref[:, m * step : (m + 1) * step] = total.astype(jnp.bfloat16)


def finish(mixed, back):
    return pl.pallas_call(
        finish_kernel,
        out_shape=jax.ShapeDtypeStruct(mixed.shape, jnp.bfloat16),
        in_specs=[VMEM, VMEM],
        out_specs=VMEM,
        compiler_params=pltpu.CompilerParams(vmem_limit_bytes=16 * 2**20),
        name="finish",
    )(mixed, back)


def on_device(
    queries,
    k_cache,
    v_cache,
    lengths,
    residual_in,
    norm_gain,
    gate_w,
    up_w,
    down_w,
    block_list,
    block_count,
):
    dev_count = lax.axis_size("hid")
    group_total = dev_count // MDL
    rows_dev = queries.shape[0]
    count = block_list.shape[1]
    units = count * gate_w.shape[3]
    masks = [chip * CORES for chip in range(CHIPS)]
    far_first = range(CHIPS - 1, 0, -1)
    gate_early = max(1, count * 4 // 7)
    up_early = max(1, count * 2 // 7)

    mixed_rows, kept, sent, listed, live, gate_near = attend(
        queries,
        k_cache,
        v_cache,
        lengths,
        residual_in,
        norm_gain,
        block_list,
        block_count,
        gate_w,
        gate_early,
    )
    pair = jnp.stack([kept, from_partner(sent, 1)], axis=1)
    came = {chip: from_partner(pair[chip], masks[chip]) for chip in far_first}
    middle = [(gate_w, gate_early, count), (up_w, 0, up_early)]
    gate_far, up_near, own = fetch(listed, middle, pair[0], "fetch_middle", True)
    arrived = jnp.stack([own] + [came[chip] for chip in range(1, CHIPS)])[None]
    (up_far,) = fetch(listed, [(up_w, up_early, count)], arrived, "fetch_up", False)
    for level in range(group_total.bit_length() - 1):
        arrived = jnp.concatenate([arrived, from_partner(arrived, MDL << level)], axis=0)

    part, sent = gate_up(arrived, (gate_near, gate_far), (up_near, up_far), live)
    part = part + from_partner(sent, 1).astype(jnp.float32)
    part = part.reshape(CHIPS, group_total * rows_dev, 2 * units)
    came = [from_partner(part[chip].astype(jnp.bfloat16), masks[chip]) for chip in far_first]
    down_rows, total = fetch(listed, [(down_w, 0, count)], part[0], "fetch_down", True)
    for piece in came:
        total = total + piece.astype(jnp.float32)
    hidden = (jnp.maximum(total[:, :units], 0.0) * total[:, units:]).astype(jnp.bfloat16)

    pieces = [hidden] * (2 * CHIPS)
    pieces[CHIPS] = from_partner(hidden, 1)
    for chip in far_first:
        pieces[chip] = from_partner(hidden, masks[chip])
        pieces[CHIPS + chip] = from_partner(pieces[chip], 1)
    ffn_part = down(pieces, down_rows, dev_count)
    returned = lax.all_to_all(ffn_part, "hid", split_axis=0, concat_axis=0, tiled=True)
    return finish(mixed_rows, returned)


def solution(mesh):
    in_specs = (
        P(("groups", "hid"), None, None),
        P(("groups", "hid"), None, None),
        P(("groups", "hid"), None, None),
        P(("groups", "hid")),
        P(("groups", "hid"), None),
        P(),
        P("hid", None, None, None),
        P("hid", None, None, None),
        P("hid", None, None, None),
        P("groups", None),
        P("groups"),
    )
    out_specs = P(("groups", "hid"), None)
    return jax.shard_map(
        on_device, mesh=mesh, in_specs=in_specs, out_specs=out_specs, check_vma=False
    )
```

```python
import functools
import math

import jax
import jax.numpy as jnp
from jax import lax
from jax.experimental import pallas as pl
from jax.experimental.pallas import tpu as pltpu
from jax.sharding import PartitionSpec as P

MDL = 8
VMEM = pl.BlockSpec(memory_space=pltpu.VMEM)
HBM = pl.BlockSpec(memory_space=pltpu.HBM)
ANY = pl.BlockSpec(memory_space=pl.ANY)


CORES = 2
CHIPS = MDL // CORES


def from_partner(value, mask):
    pairs = [(source, source ^ mask) for source in range(lax.axis_size("hid"))]
    return lax.ppermute(value, "hid", pairs)


def place():
    at = lax.axis_index("hid")
    return at // MDL, at // CORES % CHIPS, at % CORES


def in_hbm(value):
    return pltpu.with_memory_space_constraint(value, pltpu.HBM)


def block_copies(listed, w_hbm, out_ref, sems):
    return [
        pltpu.make_async_copy(w_hbm.at[0, block], out_ref.at[c], sems.at[c]) for c, block in enumerate(listed)
    ]


def attend_kernel(
    kv_count,
    len_hbm,
    q_hbm,
    k_hbm,
    v_hbm,
    res_hbm,
    gain_hbm,
    list_hbm,
    count_hbm,
    gate_hbm,
    mixed_ref,
    kept_ref,
    sent_ref,
    row_ref,
    live_ref,
    gate_ref,
    len_ref,
    q_ref,
    k_buf,
    v_buf,
    res_ref,
    gain_ref,
    list_ref,
    count_ref,
    sems,
    block_sems,
):
    rows, heads, size = q_ref.shape
    slots = k_buf.shape[1]
    width = kv_count * size
    per_kv = heads // kv_count
    lines = heads * rows
    pairs = [
        (len_hbm, len_ref),
        (q_hbm, q_ref),
        (k_hbm, k_buf),
        (v_hbm, v_buf),
        (res_hbm, res_ref),
        (gain_hbm, gain_ref),
        (list_hbm, list_ref),
        (count_hbm, count_ref),
        (list_hbm, row_ref),
    ]
    copies = [pltpu.make_async_copy(s, d, sems.at[i]) for i, (s, d) in enumerate(pairs)]
    for copy in copies[6:] + copies[:6]:
        copy.start()
    copies[6].wait()
    copies[7].wait()
    group, chip, core = place()
    early = [list_ref[group, c] for c in range(gate_ref.shape[0])]
    blocks = block_copies(early, gate_hbm, gate_ref, block_sems)
    for copy in blocks:
        copy.start()
    live_lanes = count_ref[group] * (live_ref.shape[1] // list_ref.shape[1])
    lane = lax.broadcasted_iota(jnp.int32, live_ref.shape, 1)
    live_ref[...] = (lane < live_lanes).astype(jnp.float32)
    line = lax.broadcasted_iota(jnp.int32, (lines, lines), 0)
    taken = lax.broadcasted_iota(jnp.int32, (lines, lines), 1)
    swap = (taken == line % rows * heads + line // rows).astype(jnp.float32).astype(jnp.bfloat16)
    own = (
        lax.broadcasted_iota(jnp.int32, (lines, width), 0) // (per_kv * rows)
        == lax.broadcasted_iota(jnp.int32, (lines, width), 1) // size
    )
    copies[0].wait()
    request = lax.broadcasted_iota(jnp.int32, (lines, 1), 0) % rows
    first = request * slots
    stop = first
    for r in range(rows):
        stop = jnp.where(request == r, r * slots + len_ref[r], stop)
    slot = lax.broadcasted_iota(jnp.int32, (lines, rows * slots), 1)
    valid = (slot >= first) & (slot < stop)
    copies[1].wait()
    q = jnp.dot(
        swap, q_ref[...].reshape(lines, size), preferred_element_type=jnp.float32
    ).astype(jnp.bfloat16)
    wide = jnp.where(own, jnp.concatenate([q] * kv_count, axis=1), jnp.zeros((), jnp.bfloat16))
    copies[2].wait()
    scores = lax.dot_general(
        wide,
        k_buf[...].reshape(rows * slots, width),
        (((1,), (1,)), ((), ())),
        preferred_element_type=jnp.float32,
    ) * (1.0 / math.sqrt(size))
    scores = jnp.where(valid, scores, -1e30)
    top = jnp.max(scores, axis=1, keepdims=True)
    terms = jnp.where(valid, jnp.exp(scores - top), 0.0)
    probs = (terms / jnp.sum(terms, axis=1, keepdims=True)).astype(jnp.bfloat16)
    copies[3].wait()
    values = v_buf[...].reshape(rows * slots, width)
    for j in range(kv_count):
        span = per_kv * rows
        piece = jnp.dot(
            probs[j * span : (j + 1) * span],
            values[:, j * size : (j + 1) * size],
            preferred_element_type=jnp.float32,
        )
        for i in range(per_kv):
            h = j * per_kv + i
            mixed_ref[:, h * size : (h + 1) * size] = piece[i * rows : (i + 1) * rows]
    copies[4].wait()
    copies[5].wait()
    mixed = mixed_ref[...] + res_ref[...].astype(jnp.float32)
    mixed_ref[...] = mixed
    mean_sq = jnp.mean(mixed * mixed, axis=1, keepdims=True)
    normed = (mixed * lax.rsqrt(mean_sq + 1e-05) * gain_ref[...]).astype(jnp.bfloat16)
    step = kept_ref.shape[2]
    for q in range(CHIPS):
        first = normed[:, 2 * q * step : (2 * q + 1) * step]
        second = normed[:, (2 * q + 1) * step : (2 * q + 2) * step]
        kept_ref[q ^ chip] = jnp.where(core == 0, first, second)
        sent_ref[q ^ chip] = jnp.where(core == 0, second, first)
    for copy in blocks + copies[8:]:
        copy.wait()


def attend(
    queries, k_cache, v_cache, lengths, residual_in, norm_gain, block_list, block_count, gate_w, early
):
    rows, heads, size = queries.shape
    slots, width = k_cache.shape[1:]
    model = residual_in.shape[1]
    return pl.pallas_call(
        functools.partial(attend_kernel, width // size),
        out_shape=(
            pltpu.VMEM((rows, model), jnp.float32),
            pltpu.VMEM((CHIPS, rows, model // MDL), jnp.bfloat16),
            pltpu.VMEM((CHIPS, rows, model // MDL), jnp.bfloat16),
            pltpu.VMEM(block_list.shape, jnp.int32),
            pltpu.VMEM((1, block_list.shape[1] * gate_w.shape[3]), jnp.float32),
            pltpu.VMEM((early,) + gate_w.shape[2:], jnp.bfloat16),
        ),
        in_specs=[HBM] * 9,
        out_specs=(VMEM,) * 6,
        scratch_shapes=[
            pltpu.SMEM((rows,), jnp.int32),
            pltpu.VMEM((rows, heads, size), jnp.bfloat16),
            pltpu.VMEM((rows, slots, width), jnp.bfloat16),
            pltpu.VMEM((rows, slots, width), jnp.bfloat16),
            pltpu.VMEM((rows, model), jnp.bfloat16),
            pltpu.VMEM((1, model), jnp.float32),
            pltpu.SMEM(block_list.shape, jnp.int32),
            pltpu.SMEM(block_count.shape, jnp.int32),
            pltpu.SemaphoreType.DMA((9,)),
            pltpu.SemaphoreType.DMA((early,)),
        ],
        compiler_params=pltpu.CompilerParams(vmem_limit_bytes=20 * 2**20),
        name="attend",
    )(
        *(
            in_hbm(value)
            for value in (
                lengths,
                queries,
                k_cache,
                v_cache,
                residual_in,
                norm_gain.reshape(1, model),
                block_list,
                block_count,
                gate_w,
            )
        )
    )


def fetch_kernel(firsts, rows_ref, *rest):
    parts = len(firsts)
    row = rows_ref[pl.ds(place()[0], 1), :]
    at = lax.broadcasted_iota(jnp.int32, row.shape, 1)
    copies = []
    for i, first in enumerate(firsts):
        out_ref = rest[parts + 1 + i]
        listed = [jnp.sum(jnp.where(at == first + c, row, 0)) for c in range(out_ref.shape[0])]
        copies += block_copies(listed, rest[i], out_ref, rest[-parts + i])
    for copy in copies:
        copy.start()
    for copy in copies:
        copy.wait()


def fetch(rows, parts, held, name, passed):
    out_shape = [pltpu.VMEM((stop - first,) + w.shape[2:], jnp.bfloat16) for w, first, stop in parts]
    size = 2 * sum(math.prod(blocks.shape) for blocks in out_shape)
    out_specs = [VMEM] * len(parts)
    if passed:
        out_shape.append(jax.ShapeDtypeStruct(held.shape, held.dtype))
        out_specs.append(ANY)
    return pl.pallas_call(
        functools.partial(fetch_kernel, [first for _, first, _ in parts]),
        out_shape=out_shape,
        in_specs=[VMEM] + [HBM] * len(parts) + [ANY],
        out_specs=out_specs,
        input_output_aliases={1 + len(parts): len(parts)} if passed else {},
        scratch_shapes=[pltpu.SemaphoreType.DMA((stop - first,)) for _, first, stop in parts],
        compiler_params=pltpu.CompilerParams(vmem_limit_bytes=12 * 2**20),
        cost_estimate=pl.CostEstimate(flops=0, bytes_accessed=2 * size, transcendentals=0),
        name=name,
    )(rows, *(in_hbm(w) for w, _, _ in parts), held)


def gate_up_kernel(arrived_ref, gate_near, gate_far, up_near, up_far, live_ref, *rest):
    *out_refs, x_ref = rest
    keep_refs, sent_refs = out_refs[:CHIPS], out_refs[CHIPS:]
    groups, _, _, rows, _ = arrived_ref.shape
    few = keep_refs[0].shape[0]
    unit = gate_near.shape[2]
    gates = [near_or_far.at[c] for near_or_far in (gate_near, gate_far) for c in range(near_or_far.shape[0])]
    ups = [near_or_far.at[c] for near_or_far in (up_near, up_far) for c in range(near_or_far.shape[0])]
    count = len(gates)
    for core in range(CORES):
        for chip in range(CHIPS):
            for group in range(groups):
                at = ((core * CHIPS + chip) * groups + group) * rows
                x_ref[at : at + rows, :] = arrived_ref[group, chip, core].astype(jnp.float32)
    x = x_ref[...].astype(jnp.bfloat16)
    for c in range(count):
        for k, w in enumerate((gates[c], ups[c])):
            part = jnp.dot(x, w[...], preferred_element_type=jnp.float32)
            if k == 0:
                live = live_ref[:, c * unit : (c + 1) * unit] > 0.0
                part = jnp.where(live, part, 0.0)
            at = pl.ds((k * count + c) * unit, unit)
            for chip in range(CHIPS):
                far = (CHIPS + chip) * few
                keep_refs[chip][:, at] = part[chip * few : (chip + 1) * few]
                sent_refs[chip][:, at] = part[far : far + few].astype(jnp.bfloat16)


def gate_up(arrived, gate, up, live):
    rows = math.prod(arrived.shape[:4])
    _, depth, unit = gate[0].shape
    wide = 2 * unit * sum(part.shape[0] for part in gate)
    return pl.pallas_call(
        gate_up_kernel,
        out_shape=[pltpu.VMEM((rows // MDL, wide), jnp.float32)] * CHIPS
        + [pltpu.VMEM((rows // MDL, wide), jnp.bfloat16)] * CHIPS,
        in_specs=[VMEM] * 6,
        out_specs=[VMEM] * (2 * CHIPS),
        scratch_shapes=[pltpu.VMEM((rows, depth), jnp.float32)],
        compiler_params=pltpu.CompilerParams(vmem_limit_bytes=24 * 2**20),
        name="gate_up",
    )(arrived, *gate, *up, live)


def down_kernel(*refs):
    *pieces, w_ref, out_ref = refs
    count, unit, depth = w_ref.shape
    devices, rows, _ = out_ref.shape
    groups = devices // MDL
    group, chip, core = place()
    hidden = jnp.concatenate([piece[...] for piece in pieces], axis=0)
    step = min(512, depth)
    for n in range(depth // step):
        at = pl.ds(n * step, step)
        w = w_ref[:, :, at].reshape(count * unit, step)
        total = jnp.dot(hidden, w, preferred_element_type=jnp.float32)
        for r in range(devices):
            c, q, g = r // (CHIPS * groups), r // groups % CHIPS, r % groups
            owner = (group ^ g) * MDL + (chip ^ q) * CORES + (core ^ c)
            out_ref[owner, :, at] = total[r * rows : (r + 1) * rows].astype(jnp.bfloat16)


def down(pieces, weights, devices):
    rows = sum(piece.shape[0] for piece in pieces) // devices
    return pl.pallas_call(
        down_kernel,
        out_shape=pltpu.VMEM((devices, rows, weights.shape[2]), jnp.bfloat16),
        in_specs=[VMEM] * (len(pieces) + 1),
        out_specs=VMEM,
        compiler_params=pltpu.CompilerParams(vmem_limit_bytes=20 * 2**20),
        name="down",
    )(*pieces, weights)


def finish_kernel(mixed_ref, back_ref, out_ref):
    step = back_ref.shape[2]
    for m in range(MDL):
        total = mixed_ref[:, m * step : (m + 1) * step]
        for g in range(back_ref.shape[0] // MDL):
            total = total + back_ref[g * MDL + m].astype(jnp.float32)
        out_ref[:, m * step : (m + 1) * step] = total.astype(jnp.bfloat16)


def finish(mixed, back):
    return pl.pallas_call(
        finish_kernel,
        out_shape=jax.ShapeDtypeStruct(mixed.shape, jnp.bfloat16),
        in_specs=[VMEM, VMEM],
        out_specs=VMEM,
        compiler_params=pltpu.CompilerParams(vmem_limit_bytes=16 * 2**20),
        name="finish",
    )(mixed, back)


def on_device(
    queries,
    k_cache,
    v_cache,
    lengths,
    residual_in,
    norm_gain,
    gate_w,
    up_w,
    down_w,
    block_list,
    block_count,
):
    dev_count = lax.axis_size("hid")
    group_total = dev_count // MDL
    rows_dev = queries.shape[0]
    count = block_list.shape[1]
    units = count * gate_w.shape[3]
    masks = [chip * CORES for chip in range(CHIPS)]
    far_first = range(CHIPS - 1, 0, -1)
    gate_early = max(1, count * 4 // 7)
    up_early = max(1, count * 2 // 7)

    mixed_rows, kept, sent, listed, live, gate_near = attend(
        queries,
        k_cache,
        v_cache,
        lengths,
        residual_in,
        norm_gain,
        block_list,
        block_count,
        gate_w,
        gate_early,
    )
    pair = jnp.stack([kept, from_partner(sent, 1)], axis=1)
    came = {chip: from_partner(pair[chip], masks[chip]) for chip in far_first}
    middle = [(gate_w, gate_early, count), (up_w, 0, up_early)]
    gate_far, up_near, own = fetch(listed, middle, pair[0], "fetch_middle", True)
    arrived = jnp.stack([own] + [came[chip] for chip in range(1, CHIPS)])[None]
    (up_far,) = fetch(listed, [(up_w, up_early, count)], arrived, "fetch_up", False)
    for level in range(group_total.bit_length() - 1):
        arrived = jnp.concatenate([arrived, from_partner(arrived, MDL << level)], axis=0)

    parts = gate_up(arrived, (gate_near, gate_far), (up_near, up_far), live)
    part = {}
    for chip in (*far_first, 0):
        part[chip] = parts[chip] + from_partner(parts[CHIPS + chip], 1).astype(jnp.float32)
    came = [from_partner(part[chip].astype(jnp.bfloat16), masks[chip]) for chip in far_first]
    (down_rows, total) = fetch(listed, [(down_w, 0, count)], part[0], "fetch_down", True)
    for piece in came:
        total = total + piece.astype(jnp.float32)
    hidden = (jnp.maximum(total[:, :units], 0.0) * total[:, units:]).astype(jnp.bfloat16)

    pieces = [hidden] * (2 * CHIPS)
    pieces[CHIPS] = from_partner(hidden, 1)
    for chip in far_first:
        pieces[chip] = from_partner(hidden, masks[chip])
        pieces[CHIPS + chip] = from_partner(pieces[chip], 1)
    ffn_part = down(pieces, down_rows, dev_count)
    returned = lax.all_to_all(ffn_part, "hid", split_axis=0, concat_axis=0, tiled=True)
    return finish(mixed_rows, returned)


def solution(mesh):
    in_specs = (
        P(("groups", "hid"), None, None),
        P(("groups", "hid"), None, None),
        P(("groups", "hid"), None, None),
        P(("groups", "hid")),
        P(("groups", "hid"), None),
        P(),
        P("hid", None, None, None),
        P("hid", None, None, None),
        P("hid", None, None, None),
        P("groups", None),
        P("groups"),
    )
    out_specs = P(("groups", "hid"), None)
    return jax.shard_map(
        on_device, mesh=mesh, in_specs=in_specs, out_specs=out_specs, check_vma=False
    )
```

```python
import functools
import math

import jax
import jax.numpy as jnp
from jax import lax
from jax.experimental import pallas as pl
from jax.experimental.pallas import tpu as pltpu
from jax.sharding import PartitionSpec as P

MDL = 8
VMEM = pl.BlockSpec(memory_space=pltpu.VMEM)
HBM = pl.BlockSpec(memory_space=pltpu.HBM)
ANY = pl.BlockSpec(memory_space=pl.ANY)


CORES = 2
CHIPS = MDL // CORES


def from_partner(value, mask):
    pairs = [(source, source ^ mask) for source in range(lax.axis_size("hid"))]
    return lax.ppermute(value, "hid", pairs)


def place():
    at = lax.axis_index("hid")
    return at // MDL, at // CORES % CHIPS, at % CORES


def in_hbm(value):
    return pltpu.with_memory_space_constraint(value, pltpu.HBM)


def block_copies(listed, w_hbm, out_ref, sems):
    return [
        pltpu.make_async_copy(w_hbm.at[0, block], out_ref.at[c], sems.at[c]) for c, block in enumerate(listed)
    ]


def attend_kernel(
    kv_count,
    len_hbm,
    q_hbm,
    k_hbm,
    v_hbm,
    res_hbm,
    gain_hbm,
    list_hbm,
    count_hbm,
    gate_hbm,
    mixed_ref,
    kept_ref,
    sent_ref,
    row_ref,
    live_ref,
    gate_ref,
    len_ref,
    q_ref,
    k_buf,
    v_buf,
    res_ref,
    gain_ref,
    list_ref,
    count_ref,
    sems,
    block_sems,
):
    rows, heads, size = q_ref.shape
    slots = k_buf.shape[1]
    width = kv_count * size
    per_kv = heads // kv_count
    lines = heads * rows
    pairs = [
        (len_hbm, len_ref),
        (q_hbm, q_ref),
        (k_hbm, k_buf),
        (v_hbm, v_buf),
        (res_hbm, res_ref),
        (gain_hbm, gain_ref),
        (list_hbm, list_ref),
        (count_hbm, count_ref),
        (list_hbm, row_ref),
    ]
    copies = [pltpu.make_async_copy(s, d, sems.at[i]) for i, (s, d) in enumerate(pairs)]
    for copy in copies[6:] + copies[:6]:
        copy.start()
    copies[6].wait()
    copies[7].wait()
    group, chip, core = place()
    early = [list_ref[group, c] for c in range(gate_ref.shape[0])]
    blocks = block_copies(early, gate_hbm, gate_ref, block_sems)
    for copy in blocks:
        copy.start()
    live_lanes = count_ref[group] * (live_ref.shape[1] // list_ref.shape[1])
    lane = lax.broadcasted_iota(jnp.int32, live_ref.shape, 1)
    live_ref[...] = (lane < live_lanes).astype(jnp.float32)
    line = lax.broadcasted_iota(jnp.int32, (lines, lines), 0)
    taken = lax.broadcasted_iota(jnp.int32, (lines, lines), 1)
    swap = (taken == line % rows * heads + line // rows).astype(jnp.float32).astype(jnp.bfloat16)
    own = (
        lax.broadcasted_iota(jnp.int32, (lines, width), 0) // (per_kv * rows)
        == lax.broadcasted_iota(jnp.int32, (lines, width), 1) // size
    )
    copies[0].wait()
    request = lax.broadcasted_iota(jnp.int32, (lines, 1), 0) % rows
    first = request * slots
    stop = first
    for r in range(rows):
        stop = jnp.where(request == r, r * slots + len_ref[r], stop)
    slot = lax.broadcasted_iota(jnp.int32, (lines, rows * slots), 1)
    valid = (slot >= first) & (slot < stop)
    copies[1].wait()
    q = jnp.dot(
        swap, q_ref[...].reshape(lines, size), preferred_element_type=jnp.float32
    ).astype(jnp.bfloat16)
    wide = jnp.where(own, jnp.concatenate([q] * kv_count, axis=1), jnp.zeros((), jnp.bfloat16))
    copies[2].wait()
    scores = lax.dot_general(
        wide,
        k_buf[...].reshape(rows * slots, width),
        (((1,), (1,)), ((), ())),
        preferred_element_type=jnp.float32,
    ) * (1.0 / math.sqrt(size))
    scores = jnp.where(valid, scores, -1e30)
    top = jnp.max(scores, axis=1, keepdims=True)
    terms = jnp.where(valid, jnp.exp(scores - top), 0.0)
    probs = (terms / jnp.sum(terms, axis=1, keepdims=True)).astype(jnp.bfloat16)
    copies[3].wait()
    values = v_buf[...].reshape(rows * slots, width)
    for j in range(kv_count):
        span = per_kv * rows
        piece = jnp.dot(
            probs[j * span : (j + 1) * span],
            values[:, j * size : (j + 1) * size],
            preferred_element_type=jnp.float32,
        )
        for i in range(per_kv):
            h = j * per_kv + i
            mixed_ref[:, h * size : (h + 1) * size] = piece[i * rows : (i + 1) * rows]
    copies[4].wait()
    copies[5].wait()
    mixed = mixed_ref[...] + res_ref[...].astype(jnp.float32)
    mixed_ref[...] = mixed
    mean_sq = jnp.mean(mixed * mixed, axis=1, keepdims=True)
    normed = (mixed * lax.rsqrt(mean_sq + 1e-05) * gain_ref[...]).astype(jnp.bfloat16)
    step = kept_ref.shape[2]
    for q in range(CHIPS):
        first = normed[:, 2 * q * step : (2 * q + 1) * step]
        second = normed[:, (2 * q + 1) * step : (2 * q + 2) * step]
        kept_ref[q ^ chip] = jnp.where(core == 0, first, second)
        sent_ref[q ^ chip] = jnp.where(core == 0, second, first)
    for copy in blocks + copies[8:]:
        copy.wait()


def attend(
    queries, k_cache, v_cache, lengths, residual_in, norm_gain, block_list, block_count, gate_w, early
):
    rows, heads, size = queries.shape
    slots, width = k_cache.shape[1:]
    model = residual_in.shape[1]
    return pl.pallas_call(
        functools.partial(attend_kernel, width // size),
        out_shape=(
            pltpu.VMEM((rows, model), jnp.float32),
            pltpu.VMEM((CHIPS, rows, model // MDL), jnp.bfloat16),
            pltpu.VMEM((CHIPS, rows, model // MDL), jnp.bfloat16),
            pltpu.VMEM(block_list.shape, jnp.int32),
            pltpu.VMEM((1, block_list.shape[1] * gate_w.shape[3]), jnp.float32),
            pltpu.VMEM((early,) + gate_w.shape[2:], jnp.bfloat16),
        ),
        in_specs=[HBM] * 9,
        out_specs=(VMEM,) * 6,
        scratch_shapes=[
            pltpu.SMEM((rows,), jnp.int32),
            pltpu.VMEM((rows, heads, size), jnp.bfloat16),
            pltpu.VMEM((rows, slots, width), jnp.bfloat16),
            pltpu.VMEM((rows, slots, width), jnp.bfloat16),
            pltpu.VMEM((rows, model), jnp.bfloat16),
            pltpu.VMEM((1, model), jnp.float32),
            pltpu.SMEM(block_list.shape, jnp.int32),
            pltpu.SMEM(block_count.shape, jnp.int32),
            pltpu.SemaphoreType.DMA((9,)),
            pltpu.SemaphoreType.DMA((early,)),
        ],
        compiler_params=pltpu.CompilerParams(vmem_limit_bytes=20 * 2**20),
        name="attend",
    )(
        *(
            in_hbm(value)
            for value in (
                lengths,
                queries,
                k_cache,
                v_cache,
                residual_in,
                norm_gain.reshape(1, model),
                block_list,
                block_count,
                gate_w,
            )
        )
    )


def fetch_kernel(firsts, rows_ref, *rest):
    parts = len(firsts)
    row = rows_ref[pl.ds(place()[0], 1), :]
    at = lax.broadcasted_iota(jnp.int32, row.shape, 1)
    copies = []
    for i, first in enumerate(firsts):
        out_ref = rest[parts + 1 + i]
        listed = [jnp.sum(jnp.where(at == first + c, row, 0)) for c in range(out_ref.shape[0])]
        copies += block_copies(listed, rest[i], out_ref, rest[-parts + i])
    for copy in copies:
        copy.start()
    for copy in copies:
        copy.wait()


def fetch(rows, parts, held, name, passed):
    out_shape = [pltpu.VMEM((stop - first,) + w.shape[2:], jnp.bfloat16) for w, first, stop in parts]
    size = 2 * sum(math.prod(blocks.shape) for blocks in out_shape)
    out_specs = [VMEM] * len(parts)
    if passed:
        out_shape.append(jax.ShapeDtypeStruct(held.shape, held.dtype))
        out_specs.append(ANY)
    return pl.pallas_call(
        functools.partial(fetch_kernel, [first for _, first, _ in parts]),
        out_shape=out_shape,
        in_specs=[VMEM] + [HBM] * len(parts) + [ANY],
        out_specs=out_specs,
        input_output_aliases={1 + len(parts): len(parts)} if passed else {},
        scratch_shapes=[pltpu.SemaphoreType.DMA((stop - first,)) for _, first, stop in parts],
        compiler_params=pltpu.CompilerParams(vmem_limit_bytes=14 * 2**20),
        cost_estimate=pl.CostEstimate(flops=0, bytes_accessed=2 * size, transcendentals=0),
        name=name,
    )(rows, *(in_hbm(w) for w, _, _ in parts), held)


def gate_up_kernel(levels, *refs):
    arrived, (gate_near, gate_far, up_ref, live_ref, *rest) = refs[:levels], refs[levels:]
    *out_refs, x_ref = rest
    keep_refs, sent_refs = out_refs[:CHIPS], out_refs[CHIPS:]
    arrived = [ref.at[g] for ref in arrived for g in range(ref.shape[0])]
    groups, rows = len(arrived), arrived[0].shape[2]
    few = keep_refs[0].shape[0]
    unit = gate_near.shape[2]
    gates = [near_or_far.at[c] for near_or_far in (gate_near, gate_far) for c in range(near_or_far.shape[0])]
    ups = [up_ref.at[c] for c in range(up_ref.shape[0])]
    count = len(gates)
    for core in range(CORES):
        for chip in range(CHIPS):
            for group in range(groups):
                at = ((core * CHIPS + chip) * groups + group) * rows
                x_ref[at : at + rows, :] = arrived[group][chip, core].astype(jnp.float32)
    x = x_ref[...].astype(jnp.bfloat16)
    for c in range(count):
        for k, w in enumerate((gates[c], ups[c])):
            part = jnp.dot(x, w[...], preferred_element_type=jnp.float32)
            if k == 0:
                live = live_ref[:, c * unit : (c + 1) * unit] > 0.0
                part = jnp.where(live, part, 0.0)
            at = pl.ds((k * count + c) * unit, unit)
            for chip in range(CHIPS):
                far = (CHIPS + chip) * few
                keep_refs[chip][:, at] = part[chip * few : (chip + 1) * few]
                sent_refs[chip][:, at] = part[far : far + few].astype(jnp.bfloat16)


def gate_up(arrived, gate, up, live):
    rows = sum(math.prod(level.shape[:4]) for level in arrived)
    _, depth, unit = gate[0].shape
    wide = 2 * unit * sum(part.shape[0] for part in gate)
    return pl.pallas_call(
        functools.partial(gate_up_kernel, len(arrived)),
        out_shape=[pltpu.VMEM((rows // MDL, wide), jnp.float32)] * CHIPS
        + [pltpu.VMEM((rows // MDL, wide), jnp.bfloat16)] * CHIPS,
        in_specs=[VMEM] * (len(arrived) + 4),
        out_specs=[VMEM] * (2 * CHIPS),
        scratch_shapes=[pltpu.VMEM((rows, depth), jnp.float32)],
        compiler_params=pltpu.CompilerParams(vmem_limit_bytes=24 * 2**20),
        name="gate_up",
    )(*arrived, *gate, up, live)


def down_kernel(*refs):
    *pieces, w_ref, out_ref = refs
    count, unit, depth = w_ref.shape
    devices, rows, _ = out_ref.shape
    groups = devices // MDL
    group, chip, core = place()
    hidden = jnp.concatenate([piece[...] for piece in pieces], axis=0)
    step = min(512, depth)
    for n in range(depth // step):
        at = pl.ds(n * step, step)
        w = w_ref[:, :, at].reshape(count * unit, step)
        total = jnp.dot(hidden, w, preferred_element_type=jnp.float32)
        for r in range(devices):
            c, q, g = r // (CHIPS * groups), r // groups % CHIPS, r % groups
            owner = (group ^ g) * MDL + (chip ^ q) * CORES + (core ^ c)
            out_ref[owner, :, at] = total[r * rows : (r + 1) * rows].astype(jnp.bfloat16)


def down(pieces, weights, devices):
    rows = sum(piece.shape[0] for piece in pieces) // devices
    return pl.pallas_call(
        down_kernel,
        out_shape=pltpu.VMEM((devices, rows, weights.shape[2]), jnp.bfloat16),
        in_specs=[VMEM] * (len(pieces) + 1),
        out_specs=VMEM,
        compiler_params=pltpu.CompilerParams(vmem_limit_bytes=20 * 2**20),
        name="down",
    )(*pieces, weights)


def finish_kernel(mixed_ref, back_ref, out_ref):
    step = back_ref.shape[2]
    for m in range(MDL):
        total = mixed_ref[:, m * step : (m + 1) * step]
        for g in range(back_ref.shape[0] // MDL):
            total = total + back_ref[g * MDL + m].astype(jnp.float32)
        out_ref[:, m * step : (m + 1) * step] = total.astype(jnp.bfloat16)


def finish(mixed, back):
    return pl.pallas_call(
        finish_kernel,
        out_shape=jax.ShapeDtypeStruct(mixed.shape, jnp.bfloat16),
        in_specs=[VMEM, VMEM],
        out_specs=VMEM,
        compiler_params=pltpu.CompilerParams(vmem_limit_bytes=16 * 2**20),
        name="finish",
    )(mixed, back)


def on_device(
    queries,
    k_cache,
    v_cache,
    lengths,
    residual_in,
    norm_gain,
    gate_w,
    up_w,
    down_w,
    block_list,
    block_count,
):
    dev_count = lax.axis_size("hid")
    group_total = dev_count // MDL
    rows_dev = queries.shape[0]
    count = block_list.shape[1]
    units = count * gate_w.shape[3]
    masks = [chip * CORES for chip in range(CHIPS)]
    far_first = range(CHIPS - 1, 0, -1)
    gate_early = max(1, count * 4 // 7)

    mixed_rows, kept, sent, listed, live, gate_near = attend(
        queries,
        k_cache,
        v_cache,
        lengths,
        residual_in,
        norm_gain,
        block_list,
        block_count,
        gate_w,
        gate_early,
    )
    pair = jnp.stack([kept, from_partner(sent, 1)], axis=1)
    came = {chip: from_partner(pair[chip], masks[chip]) for chip in far_first}
    arrived = jnp.stack([pair[0]] + [came[chip] for chip in range(1, CHIPS)])[None]
    later = [(gate_w, gate_early, count), (up_w, 0, count)]
    gate_far, up = fetch(listed, later, arrived, "fetch_later", False)
    levels = [arrived]
    for level in range(group_total.bit_length() - 1):
        held = levels[0] if level == 0 else jnp.concatenate(levels, axis=0)
        levels.append(from_partner(held, MDL << level))

    parts = gate_up(levels, (gate_near, gate_far), up, live)
    part = {}
    for chip in (*far_first, 0):
        part[chip] = parts[chip] + from_partner(parts[CHIPS + chip], 1).astype(jnp.float32)
    came = [from_partner(part[chip].astype(jnp.bfloat16), masks[chip]) for chip in far_first]
    (down_rows, total) = fetch(listed, [(down_w, 0, count)], part[0], "fetch_down", True)
    for piece in came:
        total = total + piece.astype(jnp.float32)
    hidden = (jnp.maximum(total[:, :units], 0.0) * total[:, units:]).astype(jnp.bfloat16)

    pieces = [hidden] * (2 * CHIPS)
    pieces[CHIPS] = from_partner(hidden, 1)
    for chip in far_first:
        pieces[chip] = from_partner(hidden, masks[chip])
        pieces[CHIPS + chip] = from_partner(pieces[chip], 1)
    ffn_part = down(pieces, down_rows, dev_count)
    returned = lax.all_to_all(ffn_part, "hid", split_axis=0, concat_axis=0, tiled=True)
    return finish(mixed_rows, returned)


def solution(mesh):
    in_specs = (
        P(("groups", "hid"), None, None),
        P(("groups", "hid"), None, None),
        P(("groups", "hid"), None, None),
        P(("groups", "hid")),
        P(("groups", "hid"), None),
        P(),
        P("hid", None, None, None),
        P("hid", None, None, None),
        P("hid", None, None, None),
        P("groups", None),
        P("groups"),
    )
    out_specs = P(("groups", "hid"), None)
    return jax.shard_map(
        on_device, mesh=mesh, in_specs=in_specs, out_specs=out_specs, check_vma=False
    )
```

```python
import functools
import math

import jax
import jax.numpy as jnp
from jax import lax
from jax.experimental import pallas as pl
from jax.experimental.pallas import tpu as pltpu
from jax.sharding import PartitionSpec as P

MDL = 8
VMEM = pl.BlockSpec(memory_space=pltpu.VMEM)
HBM = pl.BlockSpec(memory_space=pltpu.HBM)
ANY = pl.BlockSpec(memory_space=pl.ANY)


CORES = 2
CHIPS = MDL // CORES


def from_partner(value, mask):
    pairs = [(source, source ^ mask) for source in range(lax.axis_size("hid"))]
    return lax.ppermute(value, "hid", pairs)


def place():
    at = lax.axis_index("hid")
    return at // MDL, at // CORES % CHIPS, at % CORES


def in_hbm(value):
    return pltpu.with_memory_space_constraint(value, pltpu.HBM)


def block_copies(listed, w_hbm, out_ref, sems):
    return [
        pltpu.make_async_copy(w_hbm.at[0, block], out_ref.at[c], sems.at[c]) for c, block in enumerate(listed)
    ]


def attend_kernel(
    kv_count,
    len_hbm,
    q_hbm,
    k_hbm,
    v_hbm,
    res_hbm,
    gain_hbm,
    list_hbm,
    count_hbm,
    gate_hbm,
    mixed_ref,
    kept_ref,
    sent_ref,
    row_ref,
    live_ref,
    gate_ref,
    len_ref,
    q_ref,
    k_buf,
    v_buf,
    res_ref,
    gain_ref,
    list_ref,
    count_ref,
    sems,
    block_sems,
):
    rows, heads, size = q_ref.shape
    slots = k_buf.shape[1]
    width = kv_count * size
    per_kv = heads // kv_count
    lines = heads * rows
    pairs = [
        (len_hbm, len_ref),
        (q_hbm, q_ref),
        (k_hbm, k_buf),
        (v_hbm, v_buf),
        (res_hbm, res_ref),
        (gain_hbm, gain_ref),
        (list_hbm, list_ref),
        (count_hbm, count_ref),
        (list_hbm, row_ref),
    ]
    copies = [pltpu.make_async_copy(s, d, sems.at[i]) for i, (s, d) in enumerate(pairs)]
    for copy in copies[1:3] + copies[6:8] + copies[:1] + copies[3:6] + copies[8:]:
        copy.start()
    line = lax.broadcasted_iota(jnp.int32, (lines, lines), 0)
    taken = lax.broadcasted_iota(jnp.int32, (lines, lines), 1)
    swap = (taken == line % rows * heads + line // rows).astype(jnp.float32).astype(jnp.bfloat16)
    own = (
        lax.broadcasted_iota(jnp.int32, (lines, width), 0) // (per_kv * rows)
        == lax.broadcasted_iota(jnp.int32, (lines, width), 1) // size
    )
    copies[6].wait()
    copies[7].wait()
    group, chip, core = place()
    early = [list_ref[group, c] for c in range(gate_ref.shape[0])]
    blocks = block_copies(early, gate_hbm, gate_ref, block_sems)
    for copy in blocks:
        copy.start()
    live_lanes = count_ref[group] * (live_ref.shape[1] // list_ref.shape[1])
    lane = lax.broadcasted_iota(jnp.int32, live_ref.shape, 1)
    live_ref[...] = (lane < live_lanes).astype(jnp.float32)
    copies[0].wait()
    request = lax.broadcasted_iota(jnp.int32, (lines, 1), 0) % rows
    first = request * slots
    stop = first
    for r in range(rows):
        stop = jnp.where(request == r, r * slots + len_ref[r], stop)
    slot = lax.broadcasted_iota(jnp.int32, (lines, rows * slots), 1)
    valid = (slot >= first) & (slot < stop)
    copies[1].wait()
    q = jnp.dot(
        swap, q_ref[...].reshape(lines, size), preferred_element_type=jnp.float32
    ).astype(jnp.bfloat16)
    wide = jnp.where(own, jnp.concatenate([q] * kv_count, axis=1), jnp.zeros((), jnp.bfloat16))
    copies[2].wait()
    scores = lax.dot_general(
        wide,
        k_buf[...].reshape(rows * slots, width),
        (((1,), (1,)), ((), ())),
        preferred_element_type=jnp.float32,
    ) * (1.0 / math.sqrt(size))
    scores = jnp.where(valid, scores, -1e30)
    top = jnp.max(scores, axis=1, keepdims=True)
    terms = jnp.where(valid, jnp.exp(scores - top), 0.0)
    probs = (terms / jnp.sum(terms, axis=1, keepdims=True)).astype(jnp.bfloat16)
    copies[3].wait()
    values = v_buf[...].reshape(rows * slots, width)
    for j in range(kv_count):
        span = per_kv * rows
        piece = jnp.dot(
            probs[j * span : (j + 1) * span],
            values[:, j * size : (j + 1) * size],
            preferred_element_type=jnp.float32,
        )
        for i in range(per_kv):
            h = j * per_kv + i
            mixed_ref[:, h * size : (h + 1) * size] = piece[i * rows : (i + 1) * rows]
    copies[4].wait()
    copies[5].wait()
    mixed = mixed_ref[...] + res_ref[...].astype(jnp.float32)
    mixed_ref[...] = mixed
    mean_sq = jnp.mean(mixed * mixed, axis=1, keepdims=True)
    normed = (mixed * lax.rsqrt(mean_sq + 1e-05) * gain_ref[...]).astype(jnp.bfloat16)
    step = kept_ref.shape[2]
    for q in range(CHIPS):
        first = normed[:, 2 * q * step : (2 * q + 1) * step]
        second = normed[:, (2 * q + 1) * step : (2 * q + 2) * step]
        kept_ref[q ^ chip] = jnp.where(core == 0, first, second)
        sent_ref[q ^ chip] = jnp.where(core == 0, second, first)
    for copy in blocks + copies[8:]:
        copy.wait()


def attend(
    queries, k_cache, v_cache, lengths, residual_in, norm_gain, block_list, block_count, gate_w, early
):
    rows, heads, size = queries.shape
    slots, width = k_cache.shape[1:]
    model = residual_in.shape[1]
    return pl.pallas_call(
        functools.partial(attend_kernel, width // size),
        out_shape=(
            pltpu.VMEM((rows, model), jnp.float32),
            pltpu.VMEM((CHIPS, rows, model // MDL), jnp.bfloat16),
            pltpu.VMEM((CHIPS, rows, model // MDL), jnp.bfloat16),
            pltpu.VMEM(block_list.shape, jnp.int32),
            pltpu.VMEM((1, block_list.shape[1] * gate_w.shape[3]), jnp.float32),
            pltpu.VMEM((early,) + gate_w.shape[2:], jnp.bfloat16),
        ),
        in_specs=[HBM] * 9,
        out_specs=(VMEM,) * 6,
        scratch_shapes=[
            pltpu.SMEM((rows,), jnp.int32),
            pltpu.VMEM((rows, heads, size), jnp.bfloat16),
            pltpu.VMEM((rows, slots, width), jnp.bfloat16),
            pltpu.VMEM((rows, slots, width), jnp.bfloat16),
            pltpu.VMEM((rows, model), jnp.bfloat16),
            pltpu.VMEM((1, model), jnp.float32),
            pltpu.SMEM(block_list.shape, jnp.int32),
            pltpu.SMEM(block_count.shape, jnp.int32),
            pltpu.SemaphoreType.DMA((9,)),
            pltpu.SemaphoreType.DMA((early,)),
        ],
        compiler_params=pltpu.CompilerParams(vmem_limit_bytes=20 * 2**20),
        name="attend",
    )(
        *(
            in_hbm(value)
            for value in (
                lengths,
                queries,
                k_cache,
                v_cache,
                residual_in,
                norm_gain.reshape(1, model),
                block_list,
                block_count,
                gate_w,
            )
        )
    )


def fetch_kernel(firsts, rows_ref, *rest):
    parts = len(firsts)
    row = rows_ref[pl.ds(place()[0], 1), :]
    at = lax.broadcasted_iota(jnp.int32, row.shape, 1)
    copies = []
    for i, first in enumerate(firsts):
        out_ref = rest[parts + 1 + i]
        listed = [jnp.sum(jnp.where(at == first + c, row, 0)) for c in range(out_ref.shape[0])]
        copies += block_copies(listed, rest[i], out_ref, rest[-parts + i])
    for copy in copies:
        copy.start()
    for copy in copies:
        copy.wait()


def fetch(rows, parts, held, name, passed):
    out_shape = [pltpu.VMEM((stop - first,) + w.shape[2:], jnp.bfloat16) for w, first, stop in parts]
    size = 2 * sum(math.prod(blocks.shape) for blocks in out_shape)
    out_specs = [VMEM] * len(parts)
    if passed:
        out_shape.append(jax.ShapeDtypeStruct(held.shape, held.dtype))
        out_specs.append(ANY)
    return pl.pallas_call(
        functools.partial(fetch_kernel, [first for _, first, _ in parts]),
        out_shape=out_shape,
        in_specs=[VMEM] + [HBM] * len(parts) + [ANY],
        out_specs=out_specs,
        input_output_aliases={1 + len(parts): len(parts)} if passed else {},
        scratch_shapes=[pltpu.SemaphoreType.DMA((stop - first,)) for _, first, stop in parts],
        compiler_params=pltpu.CompilerParams(vmem_limit_bytes=14 * 2**20),
        cost_estimate=pl.CostEstimate(flops=0, bytes_accessed=2 * size, transcendentals=0),
        name=name,
    )(rows, *(in_hbm(w) for w, _, _ in parts), held)


def gate_up_kernel(levels, *refs):
    arrived, (gate_near, gate_far, up_ref, live_ref, *rest) = refs[:levels], refs[levels:]
    *out_refs, x_ref = rest
    keep_refs, sent_refs = out_refs[:CHIPS], out_refs[CHIPS:]
    arrived = [ref.at[g] for ref in arrived for g in range(ref.shape[0])]
    groups, rows = len(arrived), arrived[0].shape[2]
    few = keep_refs[0].shape[0]
    unit = gate_near.shape[2]
    gates = [near_or_far.at[c] for near_or_far in (gate_near, gate_far) for c in range(near_or_far.shape[0])]
    ups = [up_ref.at[c] for c in range(up_ref.shape[0])]
    count = len(gates)
    for core in range(CORES):
        for chip in range(CHIPS):
            for group in range(groups):
                at = ((core * CHIPS + chip) * groups + group) * rows
                x_ref[at : at + rows, :] = arrived[group][chip, core].astype(jnp.float32)
    x = x_ref[...].astype(jnp.bfloat16)
    for c in range(count):
        for k, w in enumerate((gates[c], ups[c])):
            part = jnp.dot(x, w[...], preferred_element_type=jnp.float32)
            if k == 0:
                live = live_ref[:, c * unit : (c + 1) * unit] > 0.0
                part = jnp.where(live, part, 0.0)
            at = pl.ds((k * count + c) * unit, unit)
            for chip in range(CHIPS):
                far = (CHIPS + chip) * few
                keep_refs[chip][:, at] = part[chip * few : (chip + 1) * few]
                sent_refs[chip][:, at] = part[far : far + few].astype(jnp.bfloat16)


def gate_up(arrived, gate, up, live):
    rows = sum(math.prod(level.shape[:4]) for level in arrived)
    _, depth, unit = gate[0].shape
    wide = 2 * unit * sum(part.shape[0] for part in gate)
    return pl.pallas_call(
        functools.partial(gate_up_kernel, len(arrived)),
        out_shape=[pltpu.VMEM((rows // MDL, wide), jnp.float32)] * CHIPS
        + [pltpu.VMEM((rows // MDL, wide), jnp.bfloat16)] * CHIPS,
        in_specs=[VMEM] * (len(arrived) + 4),
        out_specs=[VMEM] * (2 * CHIPS),
        scratch_shapes=[pltpu.VMEM((rows, depth), jnp.float32)],
        compiler_params=pltpu.CompilerParams(vmem_limit_bytes=24 * 2**20),
        name="gate_up",
    )(*arrived, *gate, up, live)


def down_kernel(*refs):
    *pieces, w_ref, out_ref = refs
    count, unit, depth = w_ref.shape
    devices, rows, _ = out_ref.shape
    groups = devices // MDL
    group, chip, core = place()
    hidden = jnp.concatenate([piece[...] for piece in pieces], axis=0)
    step = min(512, depth)
    for n in range(depth // step):
        at = pl.ds(n * step, step)
        w = w_ref[:, :, at].reshape(count * unit, step)
        total = jnp.dot(hidden, w, preferred_element_type=jnp.float32)
        for r in range(devices):
            c, q, g = r // (CHIPS * groups), r // groups % CHIPS, r % groups
            owner = (group ^ g) * MDL + (chip ^ q) * CORES + (core ^ c)
            out_ref[owner, :, at] = total[r * rows : (r + 1) * rows].astype(jnp.bfloat16)


def down(pieces, weights, devices):
    rows = sum(piece.shape[0] for piece in pieces) // devices
    return pl.pallas_call(
        down_kernel,
        out_shape=pltpu.VMEM((devices, rows, weights.shape[2]), jnp.bfloat16),
        in_specs=[VMEM] * (len(pieces) + 1),
        out_specs=VMEM,
        compiler_params=pltpu.CompilerParams(vmem_limit_bytes=20 * 2**20),
        name="down",
    )(*pieces, weights)


def finish_kernel(mixed_ref, back_ref, out_ref):
    step = back_ref.shape[2]
    for m in range(MDL):
        total = mixed_ref[:, m * step : (m + 1) * step]
        for g in range(back_ref.shape[0] // MDL):
            total = total + back_ref[g * MDL + m].astype(jnp.float32)
        out_ref[:, m * step : (m + 1) * step] = total.astype(jnp.bfloat16)


def finish(mixed, back):
    return pl.pallas_call(
        finish_kernel,
        out_shape=jax.ShapeDtypeStruct(mixed.shape, jnp.bfloat16),
        in_specs=[VMEM, VMEM],
        out_specs=VMEM,
        compiler_params=pltpu.CompilerParams(vmem_limit_bytes=16 * 2**20),
        name="finish",
    )(mixed, back)


def on_device(
    queries,
    k_cache,
    v_cache,
    lengths,
    residual_in,
    norm_gain,
    gate_w,
    up_w,
    down_w,
    block_list,
    block_count,
):
    dev_count = lax.axis_size("hid")
    group_total = dev_count // MDL
    rows_dev = queries.shape[0]
    count = block_list.shape[1]
    units = count * gate_w.shape[3]
    masks = [chip * CORES for chip in range(CHIPS)]
    far_first = range(CHIPS - 1, 0, -1)
    gate_early = max(1, count * 4 // 7)

    mixed_rows, kept, sent, listed, live, gate_near = attend(
        queries,
        k_cache,
        v_cache,
        lengths,
        residual_in,
        norm_gain,
        block_list,
        block_count,
        gate_w,
        gate_early,
    )
    pair = jnp.stack([kept, from_partner(sent, 1)], axis=1)
    came = {chip: from_partner(pair[chip], masks[chip]) for chip in far_first}
    arrived = jnp.stack([pair[0]] + [came[chip] for chip in range(1, CHIPS)])[None]
    later = [(gate_w, gate_early, count), (up_w, 0, count)]
    gate_far, up = fetch(listed, later, arrived, "fetch_later", False)
    levels = [arrived]
    for level in range(group_total.bit_length() - 1):
        held = levels[0] if level == 0 else jnp.concatenate(levels, axis=0)
        levels.append(from_partner(held, MDL << level))

    parts = gate_up(levels, (gate_near, gate_far), up, live)
    part = {}
    for chip in (*far_first, 0):
        part[chip] = parts[chip] + from_partner(parts[CHIPS + chip], 1).astype(jnp.float32)
    came = [from_partner(part[chip].astype(jnp.bfloat16), masks[chip]) for chip in far_first]
    (down_rows, total) = fetch(listed, [(down_w, 0, count)], part[0], "fetch_down", True)
    for piece in came:
        total = total + piece.astype(jnp.float32)
    hidden = (jnp.maximum(total[:, :units], 0.0) * total[:, units:]).astype(jnp.bfloat16)

    pieces = [hidden] * (2 * CHIPS)
    pieces[CHIPS] = from_partner(hidden, 1)
    for chip in far_first:
        pieces[chip] = from_partner(hidden, masks[chip])
        pieces[CHIPS + chip] = from_partner(pieces[chip], 1)
    ffn_part = down(pieces, down_rows, dev_count)
    returned = lax.all_to_all(ffn_part, "hid", split_axis=0, concat_axis=0, tiled=True)
    return finish(mixed_rows, returned)


def solution(mesh):
    in_specs = (
        P(("groups", "hid"), None, None),
        P(("groups", "hid"), None, None),
        P(("groups", "hid"), None, None),
        P(("groups", "hid")),
        P(("groups", "hid"), None),
        P(),
        P("hid", None, None, None),
        P("hid", None, None, None),
        P("hid", None, None, None),
        P("groups", None),
        P("groups"),
    )
    out_specs = P(("groups", "hid"), None)
    return jax.shard_map(
        on_device, mesh=mesh, in_specs=in_specs, out_specs=out_specs, check_vma=False
    )
```
